256 devices in a mesh: outer: 8 (over x, core), inner: 32 (over y, z).
Axes of the slice: x: 4, y: 4, z: 8, core: 2. Of those that a mesh axis runs over, the one named last changes fastest.
Arguments:
- basis: float32 [32768, 1024], P(('outer', 'inner')), may hold values from -0.1875 to 0.1875
- fields: float32 [32768, 64], P(('outer', 'inner')), may hold values from -6 to 6
- positions: int32 [32768], P(('outer', 'inner')), may hold values from 0 to 511
- nugget: float32 [32768], P(('outer', 'inner')), may hold values from 0.2 to 2
Outputs:
- posterior_mean: float32 [32768, 64], P(('outer', 'inner'))
- root_coef: float32 [512, 64], replicated
The draws below stay inside these ranges and needn't reach their ends.
All inputs are finite; a program needn't handle non-finite values.
Results may differ from the reference program's by a relative error of at most 0.0001.
Values sent between devices are 32-bit elements; how exact they have to be, the bound alone decides.
A program may use at most 64 MiB of HBM per device.

```python
import math
import jax
import jax.numpy as jnp
from jax import lax

M = 512
R = 512
K = 1024
F = 64
RANGE = 8
GRID = 512
ROWS = 32768
N_OUTER = 8
N_INNER = 32


def with_ends(array, stream_key, smallest, high):
    longest = array.shape.index(max(array.shape))
    spots = []
    for shift in (0, 1):
        where = [jax.random.randint(jax.random.fold_in(stream_key, axis), (), 0, length) for axis, length in enumerate(array.shape)]
        where[longest] = (where[longest] + shift) % array.shape[longest]
        spots.append(tuple(where))
    return array.at[spots[0]].set(smallest).at[spots[1]].set(high)


def block_scale(own_key, shape, pieces, low, top_value):
    def one(axis_at, parts):
        steps = jax.random.uniform(jax.random.fold_in(jax.random.fold_in(own_key, 6), axis_at), (parts,), jnp.float32, low / len(pieces), top_value / len(pieces))
        return jnp.repeat(jnp.exp(steps), shape[axis_at] // parts).reshape((-1,) + (1,) * (len(shape) - axis_at - 1))

    factor_of = one(*pieces[0])
    for cut in pieces[1:]:
        factor_of = factor_of * one(*cut)
    return factor_of


def normal_values(own_key, shape, width, bound, shards=(), held_as=jnp.bfloat16):
    values = jax.random.normal(own_key, shape, jnp.float32) * width
    if len(shards) > 0:
        values = block_scale(own_key, shape, shards, -0.22, 0.18) * values
    return jnp.clip(values, min=-bound, max=bound).astype(held_as)


def setup_inputs(seed: int = 0) -> dict:
    splits = jax.random.split(jax.random.key(seed), 5)
    return {
        "basis": normal_values(splits[0], (ROWS, K), K ** -0.5, 0.1875, ((0, 256),), jnp.float32),
        "fields": normal_values(splits[1], (ROWS, F), 1.0, 6.0, ((0, 256),), jnp.float32),
        "positions": with_ends(jax.random.randint(splits[2], (ROWS,), 0, GRID), jax.random.fold_in(splits[2], 1), 0, GRID - 1).astype(jnp.int32),
        "nugget": jnp.clip(jnp.exp(math.log(2.0) - 2.3025851 * jax.random.uniform(splits[3], (ROWS,), jnp.float32) ** block_scale(splits[3], (ROWS,), ((0, 256),), -0.2, 0.2)), 0.2, 2.0),
    }


def hdot(left, right):
    return jnp.dot(left, right, precision=lax.Precision.HIGHEST)

def lower_solve(factor, values):
    return lax.linalg.triangular_solve(factor, values, left_side=True, lower=True)

def factor_solve(factor, values):
    first = lax.linalg.triangular_solve(factor, values, left_side=True, lower=True)
    return lax.linalg.triangular_solve(factor, first, left_side=True, lower=True, transpose_a=True)

def whiten(basis_rows, field_rows, leaf_positions, leaf_nugget):
    distance = jnp.abs(leaf_positions[:, None] - leaf_positions[None, :]).astype(jnp.float32)
    covariance = jnp.exp(-distance / RANGE) + jnp.diag(leaf_nugget)
    factor = jnp.linalg.cholesky(covariance)
    whitened = lower_solve(factor, jnp.concatenate([basis_rows, field_rows], axis=1))
    return (whitened[:, :K], whitened[:, K:])

def reference(basis, fields, positions, nugget):
    leaves = N_OUTER * N_INNER
    per_leaf = basis.shape[0] // leaves
    field_count = fields.shape[1]
    grouped = (basis.reshape(N_OUTER, N_INNER, per_leaf, K), fields.reshape(N_OUTER, N_INNER, per_leaf, field_count), positions.reshape(N_OUTER, N_INNER, per_leaf), nugget.reshape(N_OUTER, N_INNER, per_leaf))

    def region_sums(leaf_items):

        def add_leaf(totals, leaf_item):
            white_basis, white_fields = whiten(*leaf_item)
            return ((totals[0] + hdot(white_basis.T, white_basis), totals[1] + hdot(white_basis.T, white_fields)), None)
        start_totals = (jnp.zeros((K, K), jnp.float32), jnp.zeros((K, field_count), jnp.float32))
        totals, _ = lax.scan(add_leaf, start_totals, leaf_items)
        return totals
    grams, rhs_sums = lax.map(region_sums, grouped)

    def knot_factor(gram):
        return jnp.linalg.cholesky(gram[:M, :M] + jnp.eye(M, dtype=jnp.float32))

    def eliminate(gram, rhs_sum):
        cross_block = gram[:M, M:]
        solved = factor_solve(knot_factor(gram), jnp.concatenate([cross_block, rhs_sum[:M]], axis=1))
        schur = gram[M:, M:] - hdot(cross_block.T, solved[:, :R])
        reduced = rhs_sum[M:] - hdot(cross_block.T, solved[:, R:])
        return (schur, reduced)
    schurs, reduceds = jax.vmap(eliminate)(grams, rhs_sums)
    precision_root = jnp.eye(R, dtype=jnp.float32) + jnp.sum(schurs, axis=0)
    root_coef = factor_solve(jnp.linalg.cholesky(precision_root), jnp.sum(reduceds, axis=0))

    def predict(gram, rhs_sum, region_basis):
        region_coef = factor_solve(knot_factor(gram), rhs_sum[:M] - hdot(gram[:M, M:], root_coef))
        return hdot(region_basis[:, :M], region_coef) + hdot(region_basis[:, M:], root_coef)
    means = jax.vmap(predict)(grams, rhs_sums, basis.reshape(N_OUTER, N_INNER * per_leaf, K))
    return (means.reshape(basis.shape[0], field_count), root_coef)
```

```python
import functools

import jax
import jax.numpy as jnp
from jax import lax
from jax.experimental import pallas as pl
from jax.experimental.pallas import tpu as pltpu
from jax.sharding import Mesh
from jax.sharding import PartitionSpec as P

M = 512
R = 512
K = 1024
F = 64
RANGE = 8
B = 128
PIVOTS = 8
NB = M // B
OUTER_INNER = ("outer", "inner_0", "inner_1")
PAIRS = [(i, j) for i in range(NB) for j in range(i, NB)]
TRI = {pair: at for at, pair in enumerate(PAIRS)}
A_ROWS = len(PAIRS) * B
X_ROWS = (NB * NB + NB) * B
RED_ROWS = R // 2


def dot(left, right, left_dim=1):
    return lax.dot_general(
        left,
        right,
        (((left_dim,), (0,)), ((), ())),
        precision=lax.Precision.HIGHEST,
        preferred_element_type=jnp.float32,
    )


def swept(block, n):
    def at(values, q, k):
        return values[(min(q, k), max(q, k))]

    for p in range(n):
        inverse = 1.0 / block[(p, p)]
        scaled = {q: at(block, q, p) * inverse for q in range(n) if q != p}
        new = {}
        for q in range(n):
            for k in range(q, n):
                if q == p and k == p:
                    new[(q, k)] = -inverse
                elif q == p:
                    new[(q, k)] = scaled[k]
                elif k == p:
                    new[(q, k)] = scaled[q]
                else:
                    new[(q, k)] = block[(q, k)] - scaled[q] * at(block, p, k)
        block = new
    return block


def panel(x):
    n = x.shape[0]
    b = PIVOTS
    lane = lax.broadcasted_iota(jnp.int32, (b, n), 1)
    sub = lax.broadcasted_iota(jnp.int32, (b, n), 0)
    columns = [jnp.broadcast_to(x[:, k : k + 1], (n, n)) for k in range(b)]
    block = {
        (q, k): jnp.broadcast_to(columns[k][q : q + 1, :], (b, n))
        for q in range(b)
        for k in range(q, b)
    }
    minus_inverse = swept(block, b)
    top = jnp.where(lane < b, jnp.where(lane == sub, -1.0, 0.0), x[0:b, :])
    rows = [jnp.broadcast_to(top[k : k + 1, :], (b, n)) for k in range(b)]
    minus_new = []
    for q in range(b):
        total = None
        for k in range(b):
            term = minus_inverse[(min(q, k), max(q, k))] * rows[k]
            total = term if total is None else total + term
        minus_new.append(total)
    tiles = []
    for t in range(1, n // b):
        tile = jnp.where(lane < b, 0.0, x[t * b : (t + 1) * b, :])
        for k in range(b):
            tile = tile + columns[k][t * b : (t + 1) * b, :] * minus_new[k]
        tiles.append(tile)
    first = minus_new[0]
    for q in range(1, b):
        first = jnp.where(sub == q, minus_new[q], first)
    tiles.append(-first)
    return pltpu.roll(jnp.concatenate(tiles, axis=0), n - b, 1)


def minus_inverse_of(x):
    return lax.fori_loop(0, x.shape[0] // PIVOTS, lambda _, held: panel(held), x)


def sweep_block(x_ref, new_ref, k):
    at = slice(k * B, (k + 1) * B)
    minus = minus_inverse_of(x_ref[at, at])
    new_ref[...] = -dot(minus, x_ref[at, :])
    new_ref[:, at] = minus
    new = new_ref[...]
    for i in range(NB):
        if i != k:
            rows = slice(i * B, (i + 1) * B)
            left = x_ref[at, rows]
            x_ref[rows, at] = jnp.zeros((B, B), jnp.float32)
            x_ref[rows, :] = x_ref[rows, :] - dot(left, new, 0)
    x_ref[at, :] = new


def fill_symmetric(x_ref, packed_ref):
    diagonal = lax.broadcasted_iota(jnp.int32, (B, B), 0) == lax.broadcasted_iota(
        jnp.int32, (B, B), 1
    )
    eye = jnp.where(diagonal, 1.0, 0.0)
    for (i, j), block in TRI.items():
        value = packed_ref[block * B : (block + 1) * B, :]
        ri, rj = slice(i * B, (i + 1) * B), slice(j * B, (j + 1) * B)
        if i == j:
            x_ref[ri, ri] = value + eye
        else:
            x_ref[ri, rj] = value
            x_ref[rj, ri] = value.T


def kernel(
    no,
    ny,
    nz,
    basis_ref,
    fields_ref,
    positions_ref,
    nugget_ref,
    mean_ref,
    root_ref,
    solved,
    padded,
    local_a,
    local_x,
    local_g,
    ya_in,
    yx_in,
    yg_in,
    ya,
    yx,
    yg,
    za_in,
    zx_in,
    zg_in,
    all_a,
    all_x,
    mine_g,
    knot,
    new_rows,
    weights,
    correction,
    outer_in,
    all_p,
    packed_p,
    root,
    sy,
    ry,
    sz,
    rz,
    gsz,
    grz,
    gsy,
    gry,
    so,
    ro,
):
    o = lax.axis_index("outer")
    y = lax.axis_index("inner_0")
    z = lax.axis_index("inner_1")
    me = y * nz + z
    inner = ny * nz

    def y_peer(k):
        return {"inner_0": lax.rem(y + k, ny)}

    def z_peer(k):
        return {"inner_1": lax.rem(z + k, nz)}

    def o_peer(k):
        return {"outer": lax.rem(o + k, no)}

    peers = (
        [y_peer(k) for k in range(1, ny)]
        + [z_peer(k) for k in range(1, nz)]
        + [o_peer(k) for k in range(1, no)]
    )
    barrier = pltpu.get_barrier_semaphore()
    for peer in peers:
        pl.semaphore_signal(barrier, inc=1, device_id=peer, device_id_type=pl.DeviceIdType.MESH)

    sent = []

    def send(src, dst, send_sem, recv_sem, peer):
        copy = pltpu.make_async_remote_copy(
            src_ref=src,
            dst_ref=dst,
            send_sem=send_sem,
            recv_sem=recv_sem,
            device_id=peer,
            device_id_type=pl.DeviceIdType.MESH,
        )
        copy.start()
        sent.append(copy)
        return copy

    def span(index, rows):
        return pl.ds(pl.multiple_of(index * rows, 8), rows)

    def sum_y(part, local, landing):
        rows = local.shape[0] // ny
        return [
            send(
                local.at[span(lax.rem(y + k, ny), rows)],
                landing.at[k - 1],
                sy.at[part, k - 1],
                ry.at[part, k - 1],
                y_peer(k),
            )
            for k in range(1, ny)
        ]

    def sum_z(part, held, landing):
        rows = held.shape[0] // nz
        return [
            send(
                held.at[span(lax.rem(z + k, nz), rows)],
                landing.at[k - 1],
                sz.at[part, k - 1],
                rz.at[part, k - 1],
                z_peer(k),
            )
            for k in range(1, nz)
        ]

    def gather_z(part, full):
        rows = full.shape[0] // inner
        own = full.at[span(me, rows)]
        return [
            send(own, own, gsz.at[part, k - 1], grz.at[part, k - 1], z_peer(k))
            for k in range(1, nz)
        ]

    def gather_y(part, full):
        rows = full.shape[0] // ny
        own = full.at[span(y, rows)]
        return [
            send(own, own, gsy.at[part, k - 1], gry.at[part, k - 1], y_peer(k))
            for k in range(1, ny)
        ]

    def arrived(copies):
        for copy in copies:
            copy.wait_recv()

    def summed(landing, own):
        total = own
        for k in range(landing.shape[0]):
            total = total + landing[k]
        return total

    def own_rows(ref, index, parts):
        return ref[span(index, ref.shape[0] // parts), :]

    position = jnp.broadcast_to(positions_ref[...].astype(jnp.float32), (B, B))
    diagonal = lax.broadcasted_iota(jnp.int32, (B, B), 0) == lax.broadcasted_iota(
        jnp.int32, (B, B), 1
    )
    covariance = jnp.exp(-jnp.abs(position - position.T) / RANGE) + jnp.where(
        diagonal, jnp.broadcast_to(nugget_ref[...], (B, B)), 0.0
    )
    minus = minus_inverse_of(covariance)
    solved[...] = -dot(minus, basis_ref[...])

    for i in range(NB):
        row = dot(basis_ref[:, i * B : (i + 1) * B], solved[:, i * B : M], 0)
        for j in range(i, NB):
            at = TRI[(i, j)] * B
            local_a[at : at + B, :] = row[:, (j - i) * B : (j - i + 1) * B]
    pl.semaphore_wait(barrier, len(peers))
    a_y = sum_y(0, local_a, ya_in)
    for i in range(NB):
        row = dot(basis_ref[:, i * B : (i + 1) * B], solved[:, M:], 0)
        for j in range(NB):
            at = (i * NB + j) * B
            local_x[at : at + B, :] = row[:, j * B : (j + 1) * B]
    padded[...] = jnp.zeros_like(padded)
    padded[:, 0:F] = fields_ref[...]
    left_fields = -dot(minus, padded[...])
    right_fields = pltpu.roll(left_fields, F, 1)
    for i in range(NB):
        at = (NB * NB + i) * B
        local_x[at : at + B, :] = dot(
            basis_ref[:, i * B : (i + 1) * B], left_fields, 0
        ) + dot(basis_ref[:, M + i * B : M + (i + 1) * B], right_fields, 0)
    x_y = sum_y(1, local_x, yx_in)
    arrived(a_y)
    ya[...] = summed(ya_in, own_rows(local_a, y, ny))
    a_z = sum_z(0, ya, za_in)
    for i in range(NB):
        row = dot(
            basis_ref[:, M + i * B : M + (i + 1) * B], solved[:, M + i * B :], 0
        )
        for j in range(i, NB):
            at = TRI[(i, j)] * B
            local_g[at : at + B, :] = row[:, (j - i) * B : (j - i + 1) * B]
    arrived(a_z)
    all_a[span(me, A_ROWS // inner), :] = summed(za_in, own_rows(ya, z, nz))
    a_gz = gather_z(0, all_a)
    arrived(a_gz)
    a_gy = gather_y(0, all_a)
    arrived(x_y)
    yx[...] = summed(yx_in, own_rows(local_x, y, ny))
    x_z = sum_z(1, yx, zx_in)
    g_y = sum_y(2, local_g, yg_in)
    arrived(a_gy)

    fill_symmetric(knot, all_a)
    sweep_block(knot, new_rows, 0)
    arrived(x_z)
    all_x[span(me, X_ROWS // inner), :] = summed(zx_in, own_rows(yx, z, nz))
    x_gz = gather_z(1, all_x)
    sweep_block(knot, new_rows, 1)
    arrived(x_gz)
    x_gy = gather_y(1, all_x)
    arrived(g_y)
    yg[...] = summed(yg_in, own_rows(local_g, y, ny))
    g_z = sum_z(2, yg, zg_in)
    sweep_block(knot, new_rows, 2)
    sweep_block(knot, new_rows, 3)
    arrived(g_z)
    mine_g[...] = summed(zg_in, own_rows(yg, z, nz))
    arrived(x_gy)

    for i in range(NB):
        rows = slice(i * B, (i + 1) * B)
        total = None
        for k in range(NB):
            right = jnp.concatenate(
                [all_x[(k * NB + j) * B : (k * NB + j + 1) * B, :] for j in range(NB)]
                + [all_x[(NB * NB + k) * B : (NB * NB + k + 1) * B, :]],
                axis=1,
            )
            term = dot(knot[rows, k * B : (k + 1) * B], right)
            total = term if total is None else total + term
        weights[rows, :] = -total
    reduced = []
    for i in range(NB):
        total = None
        for k in range(NB):
            left = all_x[(k * NB + i) * B : (k * NB + i + 1) * B, :]
            term = dot(left, weights[k * B : (k + 1) * B, i * B :], 0)
            total = term if total is None else total + term
        for j in range(i, NB):
            at = TRI[(i, j)] * B
            correction[at : at + B, :] = total[:, (j - i) * B : (j - i + 1) * B]
        root_rhs = pltpu.roll(all_x[(NB * NB + i) * B : (NB * NB + i + 1) * B, :], F, 1)
        reduced.append(root_rhs - total[:, (NB - i) * B :])
    lane = lax.broadcasted_iota(jnp.int32, (B, B), 1)
    for i in range(NB // 2):
        at = A_ROWS + i * B
        correction[at : at + B, :] = jnp.where(
            lane < F, reduced[i], pltpu.roll(reduced[i + NB // 2], F, 1)
        )
    a_share, r_share = A_ROWS // inner, RED_ROWS // inner
    share = a_share + r_share
    outer_in[o, 0:a_share, :] = mine_g[...] - correction[span(me, a_share), :]
    outer_in[o, a_share:share, :] = correction[
        pl.ds(pl.multiple_of(A_ROWS + me * r_share, 8), r_share), :
    ]
    outer = [
        send(outer_in.at[o], outer_in.at[o], so.at[k - 1], ro.at[k - 1], o_peer(k))
        for k in range(1, no)
    ]
    arrived(outer)
    total = outer_in[0]
    for k in range(1, no):
        total = total + outer_in[k]
    all_p[span(me, share), :] = total
    p_gz = gather_z(2, all_p)
    arrived(p_gz)
    p_gy = gather_y(2, all_p)
    arrived(p_gy)
    for d in range(inner):
        packed_p[d * a_share : (d + 1) * a_share, :] = all_p[d * share : d * share + a_share, :]
        at = A_ROWS + d * r_share
        packed_p[at : at + r_share, :] = all_p[d * share + a_share : (d + 1) * share, :]

    fill_symmetric(root, packed_p)
    for k in range(NB):
        sweep_block(root, new_rows, k)
    half = packed_p[A_ROWS:, :]
    root_coef = -dot(root[...], jnp.concatenate([half, pltpu.roll(half, F, 1)], axis=0))
    root_ref[...] = root_coef[:, 0:F]
    region_coef = weights[:, M:] - dot(weights[:, 0:M], root_coef)
    mean = dot(basis_ref[:, 0:M], region_coef) + dot(basis_ref[:, M:], root_coef)
    mean_ref[...] = mean[:, 0:F]
    for copy in sent:
        copy.wait_send()


def shards(basis, fields, positions, nugget):
    no, ny, nz = (lax.axis_size(axis) for axis in OUTER_INNER)
    inner = ny * nz
    f32 = jnp.float32

    def landing(parts, rows):
        return pltpu.VMEM((parts, rows, B), f32)

    def flat(rows):
        return pltpu.VMEM((rows, B), f32)

    share = (A_ROWS + RED_ROWS) // inner
    dma = pltpu.SemaphoreType.DMA
    scratch = (
        [pltpu.VMEM((B, K), f32), flat(B), flat(A_ROWS), flat(X_ROWS), flat(A_ROWS)]
        + [landing(ny - 1, rows // ny) for rows in (A_ROWS, X_ROWS, A_ROWS)]
        + [flat(rows // ny) for rows in (A_ROWS, X_ROWS, A_ROWS)]
        + [landing(nz - 1, rows // inner) for rows in (A_ROWS, X_ROWS, A_ROWS)]
        + [flat(A_ROWS), flat(X_ROWS), flat(A_ROWS // inner)]
        + [pltpu.VMEM((M, M), f32), pltpu.VMEM((B, M), f32), pltpu.VMEM((M, M + B), f32)]
        + [flat(A_ROWS + RED_ROWS), landing(no, share), flat(A_ROWS + RED_ROWS)]
        + [flat(A_ROWS + RED_ROWS), pltpu.VMEM((R, R), f32)]
        + [dma((3, ny - 1)), dma((3, ny - 1)), dma((3, nz - 1)), dma((3, nz - 1))]
        + [dma((3, nz - 1)), dma((3, nz - 1)), dma((3, ny - 1)), dma((3, ny - 1))]
        + [dma((no - 1,)), dma((no - 1,))]
    )
    return pl.pallas_call(
        functools.partial(kernel, no, ny, nz),
        out_shape=(
            jax.ShapeDtypeStruct((B, F), f32),
            jax.ShapeDtypeStruct((R, F), f32),
        ),
        in_specs=[pl.BlockSpec(memory_space=pltpu.VMEM)] * 4,
        out_specs=(pl.BlockSpec(memory_space=pltpu.VMEM),) * 2,
        scratch_shapes=scratch,
        compiler_params=pltpu.CompilerParams(
            collective_id=0, has_side_effects=True, vmem_limit_bytes=48 * 1024 * 1024
        ),
    )(basis, fields, positions.reshape(1, B), nugget.reshape(1, B))


def solution(mesh):
    split = Mesh(mesh.devices.reshape(mesh.shape["outer"], 4, 8), ("outer", "inner_0", "inner_1"))
    in_specs = (P(OUTER_INNER, None), P(OUTER_INNER, None), P(OUTER_INNER), P(OUTER_INNER))
    out_specs = (P(OUTER_INNER, None), P())
    return jax.shard_map(
        shards, mesh=split, in_specs=in_specs, out_specs=out_specs, check_vma=False
    )
```

```python
import functools

import jax
import jax.numpy as jnp
from jax import lax
from jax.experimental import pallas as pl
from jax.experimental.pallas import tpu as pltpu
from jax.sharding import Mesh
from jax.sharding import PartitionSpec as P

M = 512
R = 512
K = 1024
F = 64
RANGE = 8
B = 128
PIVOTS = 8
PANEL = 64
NB = M // B
OUTER_INNER = ("outer", "inner_0", "inner_1")
PAIRS = [(i, j) for i in range(NB) for j in range(i, NB)]
TRI = {pair: at for at, pair in enumerate(PAIRS)}
TRI_ROWS = len(PAIRS) * B
RED_ROWS = R // 2
TOP, REST, EARLY, LATE, ROOT = range(5)
PART_ROWS = {
    TOP: NB * B,
    REST: TRI_ROWS - NB * B,
    EARLY: (NB * NB // 2 + NB) * B,
    LATE: NB * NB // 2 * B,
    ROOT: TRI_ROWS,
}
Z_FIRST = (LATE,)


def dot(left, right, left_dim=1):
    return lax.dot_general(
        left,
        right,
        (((left_dim,), (0,)), ((), ())),
        precision=lax.Precision.HIGHEST,
        preferred_element_type=jnp.float32,
    )


def swept(block, n):
    def at(values, q, k):
        return values[(min(q, k), max(q, k))]

    for p in range(n):
        inverse = 1.0 / block[(p, p)]
        scaled = {q: at(block, q, p) * inverse for q in range(n) if q != p}
        new = {}
        for q in range(n):
            for k in range(q, n):
                if q == p and k == p:
                    new[(q, k)] = -inverse
                elif q == p:
                    new[(q, k)] = scaled[k]
                elif k == p:
                    new[(q, k)] = scaled[q]
                else:
                    new[(q, k)] = block[(q, k)] - scaled[q] * at(block, p, k)
        block = new
    return block


def tree_sum(terms):
    while len(terms) > 1:
        terms = [terms[i] + terms[i + 1] for i in range(0, len(terms), 2)]
    return terms[0]


def panel_rows(x):
    w, n = x.shape
    b = PIVOTS
    lane = lax.broadcasted_iota(jnp.int32, (b, n), 1)
    sub = lax.broadcasted_iota(jnp.int32, (b, n), 0)
    for p in range(0, w, b):
        inside = (lane >= p) & (lane < p + b)
        columns = [jnp.broadcast_to(x[:, p + k : p + k + 1], (w, n)) for k in range(b)]
        block = {
            (q, k): jnp.broadcast_to(columns[k][p + q : p + q + 1, :], (b, n))
            for q in range(b)
            for k in range(q, b)
        }
        minus_inverse = swept(block, b)
        top = jnp.where(inside, jnp.where(lane == sub + p, -1.0, 0.0), x[p : p + b, :])
        rows = [jnp.broadcast_to(top[k : k + 1, :], (b, n)) for k in range(b)]
        minus_new = [
            tree_sum([minus_inverse[(min(q, k), max(q, k))] * rows[k] for k in range(b)])
            for q in range(b)
        ]
        tiles = []
        for t in range(0, w, b):
            if t == p:
                tile = -minus_new[0]
                for q in range(1, b):
                    tile = jnp.where(sub == q, -minus_new[q], tile)
            else:
                tile = jnp.where(inside, 0.0, x[t : t + b, :]) + tree_sum(
                    [columns[k][t : t + b, :] * minus_new[k] for k in range(b)]
                )
            tiles.append(tile)
        x = jnp.concatenate(tiles, axis=0)
    return x


def half_swept(x):
    n = x.shape[0]
    new = panel_rows(x[0:PANEL, :])
    lane = lax.broadcasted_iota(jnp.int32, (n - PANEL, n), 1)
    rest = jnp.where(lane < PANEL, 0.0, x[PANEL:, :]) - dot(x[PANEL:, 0:PANEL], new)
    return pltpu.roll(jnp.concatenate([rest, new], axis=0), n - PANEL, 1)


def minus_inverse_of(x):
    return lax.fori_loop(0, x.shape[0] // PANEL, lambda _, held: half_swept(held), x)


def sweep_block(x_ref, new_ref, k):
    at = slice(k * B, (k + 1) * B)
    finish_block(x_ref, new_ref, k, minus_inverse_of(x_ref[at, at]))


def finish_block(x_ref, new_ref, k, minus):
    at = slice(k * B, (k + 1) * B)
    new_ref[...] = -dot(minus, x_ref[at, :])
    new_ref[:, at] = minus
    new = new_ref[...]
    for i in range(NB):
        if i != k:
            rows = slice(i * B, (i + 1) * B)
            left = x_ref[at, rows]
            x_ref[rows, at] = jnp.zeros((B, B), jnp.float32)
            x_ref[rows, :] = x_ref[rows, :] - dot(left, new, 0)
    x_ref[at, :] = new


def fill_symmetric(x_ref, row, blocks):
    diagonal = lax.broadcasted_iota(jnp.int32, (B, B), 0) == lax.broadcasted_iota(
        jnp.int32, (B, B), 1
    )
    eye = jnp.where(diagonal, 1.0, 0.0)
    for (i, j), at in TRI.items():
        if i not in row:
            continue
        value = blocks(at)
        ri, rj = slice(i * B, (i + 1) * B), slice(j * B, (j + 1) * B)
        if i == j:
            x_ref[ri, ri] = value + eye
        else:
            x_ref[ri, rj] = value
            x_ref[rj, ri] = value.T


def kernel(no, ny, nz, *refs):
    basis_ref, fields_ref, positions_ref, nugget_ref, mean_ref, root_ref = refs[:6]
    solved, padded = refs[6:8]
    local, first_in, held, second_in, full = (refs[8 + 5 * i : 13 + 5 * i] for i in range(5))
    knot, new_rows, weights, correction, outer_in, half_p, packed_p, root = refs[33:41]
    s1, r1, s2, r2, gs2, gr2, gs1, gr1, so, ro, psz, prz, psy, pry, psc, prc = refs[41:]
    o = lax.axis_index("outer")
    y = lax.axis_index("inner_0")
    z = lax.axis_index("inner_1")
    me = y * nz + z
    inner = ny * nz

    def y_peer(k):
        return {"inner_0": lax.rem(y + k, ny)}

    def z_peer(k):
        return {"inner_1": lax.rem(z + k, nz)}

    def o_peer(k):
        return {"outer": lax.rem(o + k, no)}

    def axes(part):
        in_y, in_z = (ny, y, y_peer), (nz, z, z_peer)
        return (in_z, in_y) if part in Z_FIRST else (in_y, in_z)

    peers = (
        [y_peer(k) for k in range(1, ny)]
        + [z_peer(k) for k in range(1, nz)]
        + [o_peer(k) for k in range(1, no)]
    )
    barrier = pltpu.get_barrier_semaphore()
    for peer in peers:
        pl.semaphore_signal(barrier, inc=1, device_id=peer, device_id_type=pl.DeviceIdType.MESH)

    sent = []

    def send(src, dst, send_sem, recv_sem, peer):
        copy = pltpu.make_async_remote_copy(
            src_ref=src,
            dst_ref=dst,
            send_sem=send_sem,
            recv_sem=recv_sem,
            device_id=peer,
            device_id_type=pl.DeviceIdType.MESH,
        )
        copy.start()
        sent.append(copy)
        return copy

    def span(index, rows):
        return pl.ds(pl.multiple_of(index * rows, 8), rows)

    def own(part):
        (n1, i1, _), (n2, i2, _) = axes(part)
        return span(i1 * n2 + i2, PART_ROWS[part] // inner)

    def summed(landing, mine):
        total = mine
        for k in range(landing.shape[0]):
            total = total + landing[k]
        return total

    def arrived(copies):
        for copy in copies:
            copy.wait_recv()

    pending = {}

    def sum_first(part):
        n, index, peer = axes(part)[0]
        rows = PART_ROWS[part] // n
        pending[part] = [
            send(
                local[part].at[span(lax.rem(index + k, n), rows)],
                first_in[part].at[k - 1],
                s1.at[part, k - 1],
                r1.at[part, k - 1],
                peer(k),
            )
            for k in range(1, n)
        ]

    def sum_second(part):
        n1, index1, _ = axes(part)[0]
        n, index, peer = axes(part)[1]
        arrived(pending[part])
        held[part][...] = summed(
            first_in[part], local[part][span(index1, PART_ROWS[part] // n1), :]
        )
        rows = PART_ROWS[part] // inner
        pending[part] = [
            send(
                held[part].at[span(lax.rem(index + k, n), rows)],
                second_in[part].at[k - 1],
                s2.at[part, k - 1],
                r2.at[part, k - 1],
                peer(k),
            )
            for k in range(1, n)
        ]

    def whole_sum(part):
        _, index, _ = axes(part)[1]
        arrived(pending[part])
        return summed(second_in[part], held[part][span(index, PART_ROWS[part] // inner), :])

    def gather_second(part):
        full[part][own(part), :] = whole_sum(part)
        n, _, peer = axes(part)[1]
        block = full[part].at[own(part)]
        pending[part] = [
            send(block, block, gs2.at[part, k - 1], gr2.at[part, k - 1], peer(k))
            for k in range(1, n)
        ]

    def gather_first(part):
        arrived(pending[part])
        n, index, peer = axes(part)[0]
        block = full[part].at[span(index, PART_ROWS[part] // n)]
        pending[part] = [
            send(block, block, gs1.at[part, k - 1], gr1.at[part, k - 1], peer(k))
            for k in range(1, n)
        ]

    def gathered(part):
        arrived(pending[part])

    def basis_block(i):
        return basis_ref[:, i * B : (i + 1) * B]

    def cross(ref_early, ref_late, k, j):
        block = k * NB + j
        late = block - NB * NB // 2
        ref, at = (ref_late, late) if late >= 0 else (ref_early, block)
        return ref.at[at * B : (at + 1) * B]

    def rhs(ref_early, k):
        at = NB * NB // 2 + k
        return ref_early.at[at * B : (at + 1) * B]

    position = jnp.broadcast_to(positions_ref[...].astype(jnp.float32), (B, B))
    diagonal = lax.broadcasted_iota(jnp.int32, (B, B), 0) == lax.broadcasted_iota(
        jnp.int32, (B, B), 1
    )
    covariance = jnp.exp(-jnp.abs(position - position.T) / RANGE) + jnp.where(
        diagonal, jnp.broadcast_to(nugget_ref[...], (B, B)), 0.0
    )
    minus = minus_inverse_of(covariance)
    solved[:, 0:M] = -dot(minus, basis_ref[:, 0:M])
    row = dot(basis_block(0), solved[:, 0:M], 0)
    for j in range(NB):
        local[TOP][j * B : (j + 1) * B, :] = row[:, j * B : (j + 1) * B]
    pl.semaphore_wait(barrier, len(peers))
    sum_first(TOP)
    for i in range(1, NB):
        row = dot(basis_block(i), solved[:, i * B : M], 0)
        for j in range(i, NB):
            at = (TRI[(i, j)] - NB) * B
            local[REST][at : at + B, :] = row[:, (j - i) * B : (j - i + 1) * B]
    sum_first(REST)
    solved[:, M:] = -dot(minus, basis_ref[:, M:])
    padded[...] = jnp.zeros_like(padded)
    padded[:, 0:F] = fields_ref[...]
    left_fields = -dot(minus, padded[...])
    right_fields = pltpu.roll(left_fields, F, 1)

    def cross_rows(k):
        row = dot(basis_block(k), solved[:, M:], 0)
        for j in range(NB):
            cross(local[EARLY], local[LATE], k, j)[...] = row[:, j * B : (j + 1) * B]

    for k in range(NB // 2):
        cross_rows(k)
    for i in range(NB):
        rhs(local[EARLY], i)[...] = dot(basis_block(i), left_fields, 0) + dot(
            basis_block(NB + i), right_fields, 0
        )
    sum_second(TOP)
    sum_first(EARLY)
    for k in range(NB // 2, NB):
        cross_rows(k)
    gather_second(TOP)
    sum_second(REST)
    gather_first(TOP)
    sum_first(LATE)
    for i in range(NB):
        row = dot(basis_block(NB + i), solved[:, M + i * B :], 0)
        for j in range(i, NB):
            at = TRI[(i, j)] * B
            local[ROOT][at : at + B, :] = row[:, (j - i) * B : (j - i + 1) * B]
    gather_second(REST)
    gathered(TOP)

    fill_symmetric(knot, (0,), lambda at: full[TOP][at * B : (at + 1) * B, :])
    minus = half_swept(knot[0:B, 0:B])
    gather_first(REST)
    sum_second(EARLY)
    minus = half_swept(minus)
    gathered(REST)
    fill_symmetric(
        knot, (1, 2, 3), lambda at: full[REST][(at - NB) * B : (at - NB + 1) * B, :]
    )
    finish_block(knot, new_rows, 0, minus)
    minus = half_swept(knot[B : 2 * B, B : 2 * B])
    sum_second(LATE)
    gather_second(EARLY)
    minus = half_swept(minus)
    finish_block(knot, new_rows, 1, minus)
    gather_second(LATE)
    gather_first(EARLY)
    sum_first(ROOT)
    minus = half_swept(knot[2 * B : 3 * B, 2 * B : 3 * B])
    gather_first(LATE)
    minus = half_swept(minus)
    finish_block(knot, new_rows, 2, minus)
    sum_second(ROOT)
    sweep_block(knot, new_rows, 3)
    gathered(EARLY)
    gathered(LATE)

    def cross_at(k, j):
        return cross(full[EARLY], full[LATE], k, j)[...]

    def rhs_at(k):
        return rhs(full[EARLY], k)[...]

    right = [
        jnp.concatenate([cross_at(k, j) for j in range(NB)] + [rhs_at(k)], axis=1)
        for k in range(NB)
    ]
    for i in range(NB):
        rows = slice(i * B, (i + 1) * B)
        weights[rows, :] = -sum(
            dot(knot[rows, k * B : (k + 1) * B], right[k]) for k in range(NB)
        )
    reduced = []
    for i in range(NB):
        total = sum(
            dot(cross_at(k, i), weights[k * B : (k + 1) * B, i * B :], 0) for k in range(NB)
        )
        for j in range(i, NB):
            at = TRI[(i, j)] * B
            correction[at : at + B, :] = total[:, (j - i) * B : (j - i + 1) * B]
        reduced.append(pltpu.roll(rhs_at(i), F, 1) - total[:, (NB - i) * B :])
    lane = lax.broadcasted_iota(jnp.int32, (B, B), 1)
    for i in range(NB // 2):
        at = TRI_ROWS + i * B
        correction[at : at + B, :] = jnp.where(
            lane < F, reduced[i], pltpu.roll(reduced[i + NB // 2], F, 1)
        )
    a_share, r_share = TRI_ROWS // inner, RED_ROWS // inner
    share = a_share + r_share
    outer_in[o, 0:a_share, :] = whole_sum(ROOT) - correction[span(me, a_share), :]
    outer_in[o, a_share:share, :] = correction[
        pl.ds(pl.multiple_of(TRI_ROWS + me * r_share, 8), r_share), :
    ]
    arrived(
        [
            send(outer_in.at[o], outer_in.at[o], so.at[k - 1], ro.at[k - 1], o_peer(k))
            for k in range(1, no)
        ]
    )

    core = lax.rem(o, 2)
    sibling = {"outer": o + 1 - 2 * core}
    h = share // 2
    mine = pl.ds(pl.multiple_of(core * h, 8), h)
    total = outer_in[0, mine, :]
    for k in range(1, no):
        total = total + outer_in[k, mine, :]
    half_p[core, span(me, h), :] = total
    block = half_p.at[core, span(me, h)]
    arrived(
        [
            send(block, block, psz.at[k - 1], prz.at[k - 1], z_peer(k))
            for k in range(1, nz)
        ]
    )
    block = half_p.at[core, span(y, h * nz)]
    over_y = [
        send(block, block, psy.at[k - 1], pry.at[k - 1], y_peer(k)) for k in range(1, ny)
    ]
    swaps = [send(block, block, psc.at[0], prc.at[0], sibling)]
    for k in range(1, ny):
        over_y[k - 1].wait_recv()
        block = half_p.at[core, span(lax.rem(y + ny - k, ny), h * nz)]
        swaps.append(send(block, block, psc.at[k], prc.at[k], sibling))
    arrived(swaps)
    for d in range(inner):
        for c in range(2):
            lo, hi = c * h, min((c + 1) * h, a_share)
            packed_p[d * a_share + lo : d * a_share + hi, :] = half_p[
                c, d * h : d * h + hi - lo, :
            ]
        at = TRI_ROWS + d * r_share
        packed_p[at : at + r_share, :] = half_p[1, (d + 1) * h - r_share : (d + 1) * h, :]

    fill_symmetric(root, range(NB), lambda at: packed_p[at * B : (at + 1) * B, :])
    for k in range(NB):
        sweep_block(root, new_rows, k)
    half = packed_p[TRI_ROWS:, :]
    root_coef = -dot(root[...], jnp.concatenate([half, pltpu.roll(half, F, 1)], axis=0))
    root_ref[...] = root_coef[:, 0:F]
    region_coef = weights[:, M:] - dot(weights[:, 0:M], root_coef)
    mean = dot(basis_ref[:, 0:M], region_coef) + dot(basis_ref[:, M:], root_coef)
    mean_ref[...] = mean[:, 0:F]
    for copy in sent:
        copy.wait_send()


def shards(basis, fields, positions, nugget):
    no, ny, nz = (lax.axis_size(axis) for axis in OUTER_INNER)
    inner = ny * nz
    f32 = jnp.float32

    def landing(parts, rows):
        return pltpu.VMEM((parts, rows, B), f32)

    def flat(rows):
        return pltpu.VMEM((rows, B), f32)

    share = (TRI_ROWS + RED_ROWS) // inner
    dma = pltpu.SemaphoreType.DMA
    parts = list(PART_ROWS.items())
    first = [nz if part in Z_FIRST else ny for part, _ in parts]
    widest = max(ny, nz) - 1
    scratch = (
        [pltpu.VMEM((B, K), f32), flat(B)]
        + [flat(rows) for _, rows in parts]
        + [landing(n - 1, rows // n) for n, (_, rows) in zip(first, parts)]
        + [flat(rows // n) for n, (_, rows) in zip(first, parts)]
        + [landing(inner // n - 1, rows // inner) for n, (_, rows) in zip(first, parts)]
        + [flat(rows if part != ROOT else B) for part, rows in parts]
        + [pltpu.VMEM((M, M), f32), pltpu.VMEM((B, M), f32), pltpu.VMEM((M, M + B), f32)]
        + [flat(TRI_ROWS + RED_ROWS), landing(no, share), landing(2, share // 2 * inner)]
        + [flat(TRI_ROWS + RED_ROWS), pltpu.VMEM((R, R), f32)]
        + [dma((len(parts), widest))] * 8
        + [dma((no - 1,))] * 2
        + [dma((nz - 1,))] * 2
        + [dma((ny - 1,))] * 2
        + [dma((ny,))] * 2
    )
    return pl.pallas_call(
        functools.partial(kernel, no, ny, nz),
        out_shape=(
            jax.ShapeDtypeStruct((B, F), f32),
            jax.ShapeDtypeStruct((R, F), f32),
        ),
        in_specs=[pl.BlockSpec(memory_space=pltpu.VMEM)] * 4,
        out_specs=(pl.BlockSpec(memory_space=pltpu.VMEM),) * 2,
        scratch_shapes=scratch,
        compiler_params=pltpu.CompilerParams(
            collective_id=0, has_side_effects=True, vmem_limit_bytes=48 * 1024 * 1024
        ),
    )(basis, fields, positions.reshape(1, B), nugget.reshape(1, B))


def solution(mesh):
    split = Mesh(mesh.devices.reshape(mesh.shape["outer"], 4, 8), ("outer", "inner_0", "inner_1"))
    in_specs = (P(OUTER_INNER, None), P(OUTER_INNER, None), P(OUTER_INNER), P(OUTER_INNER))
    out_specs = (P(OUTER_INNER, None), P())
    return jax.shard_map(
        shards, mesh=split, in_specs=in_specs, out_specs=out_specs, check_vma=False
    )
```

```python
import functools

import jax
import jax.numpy as jnp
from jax import lax
from jax.experimental import pallas as pl
from jax.experimental.pallas import tpu as pltpu
from jax.sharding import Mesh
from jax.sharding import PartitionSpec as P

M = 512
R = 512
K = 1024
F = 64
RANGE = 8
B = 128
PIVOTS = 8
PANEL = 64
NB = M // B
OUTER_INNER = ("outer", "inner_0", "inner_1")
PAIRS = [(i, j) for i in range(NB) for j in range(i, NB)]
TRI = {pair: at for at, pair in enumerate(PAIRS)}
TRI_ROWS = len(PAIRS) * B
RED_ROWS = R // 2
TOP, REST, EARLY, LATE, ROOT = range(5)
PART_ROWS = {
    TOP: NB * B,
    REST: TRI_ROWS - NB * B,
    EARLY: (NB * NB // 2 + NB) * B,
    LATE: NB * NB // 2 * B,
    ROOT: TRI_ROWS,
}
Z_FIRST = (LATE,)


def dot(left, right, left_dim=1):
    return lax.dot_general(
        left,
        right,
        (((left_dim,), (0,)), ((), ())),
        precision=lax.Precision.HIGHEST,
        preferred_element_type=jnp.float32,
    )


def halves(x):
    high = x.astype(jnp.bfloat16)
    return high, (x - high.astype(jnp.float32)).astype(jnp.bfloat16)


def dot3(left, right, left_dim=1):
    left = left if isinstance(left, tuple) else halves(left)
    right = right if isinstance(right, tuple) else halves(right)

    def one(a, b):
        return lax.dot_general(
            a, b, (((left_dim,), (0,)), ((), ())), preferred_element_type=jnp.float32
        )

    return one(left[0], right[0]) + (one(left[0], right[1]) + one(left[1], right[0]))


def swept(block, n):
    def at(values, q, k):
        return values[(min(q, k), max(q, k))]

    for p in range(n):
        inverse = 1.0 / block[(p, p)]
        scaled = {q: at(block, q, p) * inverse for q in range(n) if q != p}
        new = {}
        for q in range(n):
            for k in range(q, n):
                if q == p and k == p:
                    new[(q, k)] = -inverse
                elif q == p:
                    new[(q, k)] = scaled[k]
                elif k == p:
                    new[(q, k)] = scaled[q]
                else:
                    new[(q, k)] = block[(q, k)] - scaled[q] * at(block, p, k)
        block = new
    return block


def tree_sum(terms):
    while len(terms) > 1:
        terms = [terms[i] + terms[i + 1] for i in range(0, len(terms), 2)]
    return terms[0]


def panel_rows(x):
    w, n = x.shape
    b = PIVOTS
    lane = lax.broadcasted_iota(jnp.int32, (b, n), 1)
    sub = lax.broadcasted_iota(jnp.int32, (b, n), 0)
    for p in range(0, w, b):
        inside = (lane >= p) & (lane < p + b)
        columns = [jnp.broadcast_to(x[:, p + k : p + k + 1], (w, n)) for k in range(b)]
        block = {
            (q, k): jnp.broadcast_to(columns[k][p + q : p + q + 1, :], (b, n))
            for q in range(b)
            for k in range(q, b)
        }
        minus_inverse = swept(block, b)
        top = jnp.where(inside, jnp.where(lane == sub + p, -1.0, 0.0), x[p : p + b, :])
        rows = [jnp.broadcast_to(top[k : k + 1, :], (b, n)) for k in range(b)]
        minus_new = [
            tree_sum([minus_inverse[(min(q, k), max(q, k))] * rows[k] for k in range(b)])
            for q in range(b)
        ]
        tiles = []
        for t in range(0, w, b):
            if t == p:
                tile = -minus_new[0]
                for q in range(1, b):
                    tile = jnp.where(sub == q, -minus_new[q], tile)
            else:
                tile = jnp.where(inside, 0.0, x[t : t + b, :]) + tree_sum(
                    [columns[k][t : t + b, :] * minus_new[k] for k in range(b)]
                )
            tiles.append(tile)
        x = jnp.concatenate(tiles, axis=0)
    return x


def half_swept(x):
    n = x.shape[0]
    new = panel_rows(x[0:PANEL, :])
    lane = lax.broadcasted_iota(jnp.int32, (n - PANEL, n), 1)
    rest = jnp.where(lane < PANEL, 0.0, x[PANEL:, :]) - dot(x[PANEL:, 0:PANEL], new)
    return pltpu.roll(jnp.concatenate([rest, new], axis=0), n - PANEL, 1)


def minus_inverse_of(x):
    return lax.fori_loop(0, x.shape[0] // PANEL, lambda _, held: half_swept(held), x)


def sweep_block(x_ref, new_ref, k):
    at = slice(k * B, (k + 1) * B)
    finish_block(x_ref, new_ref, k, minus_inverse_of(x_ref[at, at]))


def finish_block(x_ref, new_ref, k, minus):
    at = slice(k * B, (k + 1) * B)
    row = halves(x_ref[at, :])
    new_ref[...] = -dot3(minus, row)
    new_ref[:, at] = minus
    new = new_ref[...]
    right = halves(new)
    for i in range(NB):
        if i != k:
            rows = slice(i * B, (i + 1) * B)
            x_ref[rows, at] = jnp.zeros((B, B), jnp.float32)
            x_ref[rows, :] = x_ref[rows, :] - dot3(tuple(h[:, rows] for h in row), right, 0)
    x_ref[at, :] = new


def fill_symmetric(x_ref, row, blocks):
    diagonal = lax.broadcasted_iota(jnp.int32, (B, B), 0) == lax.broadcasted_iota(
        jnp.int32, (B, B), 1
    )
    eye = jnp.where(diagonal, 1.0, 0.0)
    for (i, j), at in TRI.items():
        if i not in row:
            continue
        value = blocks(at)
        ri, rj = slice(i * B, (i + 1) * B), slice(j * B, (j + 1) * B)
        if i == j:
            x_ref[ri, ri] = value + eye
        else:
            x_ref[ri, rj] = value
            x_ref[rj, ri] = value.T


def kernel(no, ny, nz, *refs):
    basis_ref, fields_ref, positions_ref, nugget_ref, mean_ref, root_ref = refs[:6]
    solved, padded = refs[6:8]
    local, first_in, held, second_in, full = (refs[8 + 5 * i : 13 + 5 * i] for i in range(5))
    knot, new_rows, weights, correction, outer_in, half_p, packed_p, root = refs[33:41]
    s1, r1, s2, r2, gs2, gr2, gs1, gr1, so, ro, psz, prz, psy, pry, psc, prc = refs[41:]
    o = lax.axis_index("outer")
    y = lax.axis_index("inner_0")
    z = lax.axis_index("inner_1")
    me = y * nz + z
    inner = ny * nz

    def y_peer(k):
        return {"inner_0": lax.rem(y + k, ny)}

    def z_peer(k):
        return {"inner_1": lax.rem(z + k, nz)}

    def o_peer(k):
        return {"outer": lax.rem(o + k, no)}

    def axes(part):
        in_y, in_z = (ny, y, y_peer), (nz, z, z_peer)
        return (in_z, in_y) if part in Z_FIRST else (in_y, in_z)

    peers = (
        [y_peer(k) for k in range(1, ny)]
        + [z_peer(k) for k in range(1, nz)]
        + [o_peer(k) for k in range(1, no)]
    )
    barrier = pltpu.get_barrier_semaphore()
    for peer in peers:
        pl.semaphore_signal(barrier, inc=1, device_id=peer, device_id_type=pl.DeviceIdType.MESH)

    sent = []

    def send(src, dst, send_sem, recv_sem, peer):
        copy = pltpu.make_async_remote_copy(
            src_ref=src,
            dst_ref=dst,
            send_sem=send_sem,
            recv_sem=recv_sem,
            device_id=peer,
            device_id_type=pl.DeviceIdType.MESH,
        )
        copy.start()
        sent.append(copy)
        return copy

    def span(index, rows):
        return pl.ds(pl.multiple_of(index * rows, 8), rows)

    def own(part):
        (n1, i1, _), (n2, i2, _) = axes(part)
        return span(i1 * n2 + i2, PART_ROWS[part] // inner)

    def summed(landing, mine):
        total = mine
        for k in range(landing.shape[0]):
            total = total + landing[k]
        return total

    def arrived(copies):
        for copy in copies:
            copy.wait_recv()

    pending = {}

    def sum_first(part):
        n, index, peer = axes(part)[0]
        rows = PART_ROWS[part] // n
        pending[part] = [
            send(
                local[part].at[span(lax.rem(index + k, n), rows)],
                first_in[part].at[k - 1],
                s1.at[part, k - 1],
                r1.at[part, k - 1],
                peer(k),
            )
            for k in range(1, n)
        ]

    def sum_second(part):
        n1, index1, _ = axes(part)[0]
        n, index, peer = axes(part)[1]
        arrived(pending[part])
        held[part][...] = summed(
            first_in[part], local[part][span(index1, PART_ROWS[part] // n1), :]
        )
        rows = PART_ROWS[part] // inner
        pending[part] = [
            send(
                held[part].at[span(lax.rem(index + k, n), rows)],
                second_in[part].at[k - 1],
                s2.at[part, k - 1],
                r2.at[part, k - 1],
                peer(k),
            )
            for k in range(1, n)
        ]

    def whole_sum(part):
        _, index, _ = axes(part)[1]
        arrived(pending[part])
        return summed(second_in[part], held[part][span(index, PART_ROWS[part] // inner), :])

    def gather_second(part):
        full[part][own(part), :] = whole_sum(part)
        n, _, peer = axes(part)[1]
        block = full[part].at[own(part)]
        pending[part] = [
            send(block, block, gs2.at[part, k - 1], gr2.at[part, k - 1], peer(k))
            for k in range(1, n)
        ]

    def gather_first(part):
        arrived(pending[part])
        n, index, peer = axes(part)[0]
        block = full[part].at[span(index, PART_ROWS[part] // n)]
        pending[part] = [
            send(block, block, gs1.at[part, k - 1], gr1.at[part, k - 1], peer(k))
            for k in range(1, n)
        ]

    def gathered(part):
        arrived(pending[part])

    def basis_block(i):
        return basis_ref[:, i * B : (i + 1) * B]

    def cross(ref_early, ref_late, k, j):
        block = k * NB + j
        late = block - NB * NB // 2
        ref, at = (ref_late, late) if late >= 0 else (ref_early, block)
        return ref.at[at * B : (at + 1) * B]

    def rhs(ref_early, k):
        at = NB * NB // 2 + k
        return ref_early.at[at * B : (at + 1) * B]

    position = jnp.broadcast_to(positions_ref[...].astype(jnp.float32), (B, B))
    diagonal = lax.broadcasted_iota(jnp.int32, (B, B), 0) == lax.broadcasted_iota(
        jnp.int32, (B, B), 1
    )
    covariance = jnp.exp(-jnp.abs(position - position.T) / RANGE) + jnp.where(
        diagonal, jnp.broadcast_to(nugget_ref[...], (B, B)), 0.0
    )
    minus = minus_inverse_of(covariance)
    solved[:, 0:M] = -dot3(minus, basis_ref[:, 0:M])
    row = dot3(basis_block(0), solved[:, 0:M], 0)
    for j in range(NB):
        local[TOP][j * B : (j + 1) * B, :] = row[:, j * B : (j + 1) * B]
    pl.semaphore_wait(barrier, len(peers))
    sum_first(TOP)
    for i in range(1, NB):
        row = dot3(basis_block(i), solved[:, i * B : M], 0)
        for j in range(i, NB):
            at = (TRI[(i, j)] - NB) * B
            local[REST][at : at + B, :] = row[:, (j - i) * B : (j - i + 1) * B]
    sum_first(REST)
    solved[:, M:] = -dot3(minus, basis_ref[:, M:])
    padded[...] = jnp.zeros_like(padded)
    padded[:, 0:F] = fields_ref[...]
    left_fields = -dot3(minus, padded[...])
    right_fields = pltpu.roll(left_fields, F, 1)

    def cross_rows(k):
        row = dot3(basis_block(k), solved[:, M:], 0)
        for j in range(NB):
            cross(local[EARLY], local[LATE], k, j)[...] = row[:, j * B : (j + 1) * B]

    for k in range(NB // 2):
        cross_rows(k)
    for i in range(NB):
        rhs(local[EARLY], i)[...] = dot3(basis_block(i), left_fields, 0) + dot3(
            basis_block(NB + i), right_fields, 0
        )
    sum_second(TOP)
    for k in range(NB // 2, NB):
        cross_rows(k)
    gather_second(TOP)
    sum_second(REST)
    gather_first(TOP)
    for i in range(NB):
        row = dot3(basis_block(NB + i), solved[:, M + i * B :], 0)
        for j in range(i, NB):
            at = TRI[(i, j)] * B
            local[ROOT][at : at + B, :] = row[:, (j - i) * B : (j - i + 1) * B]
    gather_second(REST)
    gathered(TOP)
    gather_first(REST)
    sum_first(EARLY)
    sum_first(LATE)

    fill_symmetric(knot, (0,), lambda at: full[TOP][at * B : (at + 1) * B, :])
    minus = half_swept(knot[0:B, 0:B])
    minus = half_swept(minus)
    gathered(REST)
    fill_symmetric(
        knot, (1, 2, 3), lambda at: full[REST][(at - NB) * B : (at - NB + 1) * B, :]
    )
    finish_block(knot, new_rows, 0, minus)
    minus = half_swept(knot[B : 2 * B, B : 2 * B])
    sum_second(EARLY)
    sum_second(LATE)
    minus = half_swept(minus)
    finish_block(knot, new_rows, 1, minus)
    gather_second(EARLY)
    gather_second(LATE)
    minus = half_swept(knot[2 * B : 3 * B, 2 * B : 3 * B])
    gather_first(LATE)
    gather_first(EARLY)
    sum_first(ROOT)
    minus = half_swept(minus)
    finish_block(knot, new_rows, 2, minus)
    minus = half_swept(knot[3 * B :, 3 * B :])
    sum_second(ROOT)
    minus = half_swept(minus)
    finish_block(knot, new_rows, 3, minus)
    gathered(EARLY)
    gathered(LATE)

    def cross_at(k, j):
        return cross(full[EARLY], full[LATE], k, j)[...]

    def rhs_at(k):
        return rhs(full[EARLY], k)[...]

    right = halves(
        jnp.concatenate(
            [
                jnp.concatenate([cross_at(k, j) for j in range(NB)] + [rhs_at(k)], axis=1)
                for k in range(NB)
            ],
            axis=0,
        )
    )
    weights[...] = -dot3(knot[...], right)
    solved_cross = halves(weights[...])
    reduced = []
    for i in range(NB):
        total = dot3(
            tuple(h[:, i * B : (i + 1) * B] for h in right),
            tuple(h[:, i * B :] for h in solved_cross),
            0,
        )
        for j in range(i, NB):
            at = TRI[(i, j)] * B
            correction[at : at + B, :] = total[:, (j - i) * B : (j - i + 1) * B]
        reduced.append(pltpu.roll(rhs_at(i), F, 1) - total[:, (NB - i) * B :])
    lane = lax.broadcasted_iota(jnp.int32, (B, B), 1)
    for i in range(NB // 2):
        at = TRI_ROWS + i * B
        correction[at : at + B, :] = jnp.where(
            lane < F, reduced[i], pltpu.roll(reduced[i + NB // 2], F, 1)
        )
    a_share, r_share = TRI_ROWS // inner, RED_ROWS // inner
    share = a_share + r_share
    outer_in[o, 0:a_share, :] = whole_sum(ROOT) - correction[span(me, a_share), :]
    outer_in[o, a_share:share, :] = correction[
        pl.ds(pl.multiple_of(TRI_ROWS + me * r_share, 8), r_share), :
    ]
    arrived(
        [
            send(outer_in.at[o], outer_in.at[o], so.at[k - 1], ro.at[k - 1], o_peer(k))
            for k in range(1, no)
        ]
    )

    core = lax.rem(o, 2)
    sibling = {"outer": o + 1 - 2 * core}
    h = share // 2
    mine = pl.ds(pl.multiple_of(core * h, 8), h)
    total = outer_in[0, mine, :]
    for k in range(1, no):
        total = total + outer_in[k, mine, :]
    half_p[core, span(me, h), :] = total
    block = half_p.at[core, span(me, h)]
    arrived(
        [
            send(block, block, psz.at[k - 1], prz.at[k - 1], z_peer(k))
            for k in range(1, nz)
        ]
    )
    block = half_p.at[core, span(y, h * nz)]
    over_y = [
        send(block, block, psy.at[k - 1], pry.at[k - 1], y_peer(k)) for k in range(1, ny)
    ]
    swaps = [send(block, block, psc.at[0], prc.at[0], sibling)]
    for k in range(1, ny):
        over_y[k - 1].wait_recv()
        block = half_p.at[core, span(lax.rem(y + ny - k, ny), h * nz)]
        swaps.append(send(block, block, psc.at[k], prc.at[k], sibling))
    arrived(swaps)
    for d in range(inner):
        for c in range(2):
            lo, hi = c * h, min((c + 1) * h, a_share)
            packed_p[d * a_share + lo : d * a_share + hi, :] = half_p[
                c, d * h : d * h + hi - lo, :
            ]
        at = TRI_ROWS + d * r_share
        packed_p[at : at + r_share, :] = half_p[1, (d + 1) * h - r_share : (d + 1) * h, :]

    fill_symmetric(root, range(NB), lambda at: packed_p[at * B : (at + 1) * B, :])
    for k in range(NB):
        sweep_block(root, new_rows, k)
    half = packed_p[TRI_ROWS:, :]
    root_coef = -dot3(root[...], jnp.concatenate([half, pltpu.roll(half, F, 1)], axis=0))
    root_ref[...] = root_coef[:, 0:F]
    region_coef = weights[:, M:] - dot3(weights[:, 0:M], root_coef)
    mean = dot3(basis_ref[:, 0:M], region_coef) + dot3(basis_ref[:, M:], root_coef)
    mean_ref[...] = mean[:, 0:F]
    for copy in sent:
        copy.wait_send()


def shards(basis, fields, positions, nugget):
    no, ny, nz = (lax.axis_size(axis) for axis in OUTER_INNER)
    inner = ny * nz
    f32 = jnp.float32

    def landing(parts, rows):
        return pltpu.VMEM((parts, rows, B), f32)

    def flat(rows):
        return pltpu.VMEM((rows, B), f32)

    share = (TRI_ROWS + RED_ROWS) // inner
    dma = pltpu.SemaphoreType.DMA
    parts = list(PART_ROWS.items())
    first = [nz if part in Z_FIRST else ny for part, _ in parts]
    widest = max(ny, nz) - 1
    scratch = (
        [pltpu.VMEM((B, K), f32), flat(B)]
        + [flat(rows) for _, rows in parts]
        + [landing(n - 1, rows // n) for n, (_, rows) in zip(first, parts)]
        + [flat(rows // n) for n, (_, rows) in zip(first, parts)]
        + [landing(inner // n - 1, rows // inner) for n, (_, rows) in zip(first, parts)]
        + [flat(rows if part != ROOT else B) for part, rows in parts]
        + [pltpu.VMEM((M, M), f32), pltpu.VMEM((B, M), f32), pltpu.VMEM((M, M + B), f32)]
        + [flat(TRI_ROWS + RED_ROWS), landing(no, share), landing(2, share // 2 * inner)]
        + [flat(TRI_ROWS + RED_ROWS), pltpu.VMEM((R, R), f32)]
        + [dma((len(parts), widest))] * 8
        + [dma((no - 1,))] * 2
        + [dma((nz - 1,))] * 2
        + [dma((ny - 1,))] * 2
        + [dma((ny,))] * 2
    )
    return pl.pallas_call(
        functools.partial(kernel, no, ny, nz),
        out_shape=(
            jax.ShapeDtypeStruct((B, F), f32),
            jax.ShapeDtypeStruct((R, F), f32),
        ),
        in_specs=[pl.BlockSpec(memory_space=pltpu.VMEM)] * 4,
        out_specs=(pl.BlockSpec(memory_space=pltpu.VMEM),) * 2,
        scratch_shapes=scratch,
        compiler_params=pltpu.CompilerParams(
            collective_id=0, has_side_effects=True, vmem_limit_bytes=48 * 1024 * 1024
        ),
    )(basis, fields, positions.reshape(1, B), nugget.reshape(1, B))


def solution(mesh):
    split = Mesh(mesh.devices.reshape(mesh.shape["outer"], 4, 8), ("outer", "inner_0", "inner_1"))
    in_specs = (P(OUTER_INNER, None), P(OUTER_INNER, None), P(OUTER_INNER), P(OUTER_INNER))
    out_specs = (P(OUTER_INNER, None), P())
    return jax.shard_map(
        shards, mesh=split, in_specs=in_specs, out_specs=out_specs, check_vma=False
    )
```

```python
import functools

import jax
import jax.numpy as jnp
from jax import lax
from jax.experimental import pallas as pl
from jax.experimental.pallas import tpu as pltpu
from jax.sharding import Mesh
from jax.sharding import PartitionSpec as P

M = 512
R = 512
K = 1024
F = 64
RANGE = 8
B = 128
PIVOTS = 8
PANEL = 64
NB = M // B
OUTER_INNER = ("outer", "inner_0", "inner_1")
PAIRS = [(i, j) for i in range(NB) for j in range(i, NB)]
TRI = {pair: at for at, pair in enumerate(PAIRS)}
TRI_ROWS = len(PAIRS) * B
RED_ROWS = R // 2
TOP, REST, EARLY, LATE, ROOT = range(5)
PART_ROWS = {
    TOP: NB * B,
    REST: TRI_ROWS - NB * B,
    EARLY: (NB * NB // 2 + NB) * B,
    LATE: NB * NB // 2 * B,
    ROOT: TRI_ROWS,
}
Z_FIRST = (LATE,)


def dot(left, right, left_dim=1):
    return lax.dot_general(
        left,
        right,
        (((left_dim,), (0,)), ((), ())),
        precision=lax.Precision.HIGHEST,
        preferred_element_type=jnp.float32,
    )


def halves(x):
    high = x.astype(jnp.bfloat16)
    return high, (x - high.astype(jnp.float32)).astype(jnp.bfloat16)


def dot3(left, right, left_dim=1):
    left = left if isinstance(left, tuple) else halves(left)
    right = right if isinstance(right, tuple) else halves(right)

    def one(a, b):
        return lax.dot_general(
            a, b, (((left_dim,), (0,)), ((), ())), preferred_element_type=jnp.float32
        )

    return one(left[0], right[0]) + (one(left[0], right[1]) + one(left[1], right[0]))


def swept(block, n):
    def at(values, q, k):
        return values[(min(q, k), max(q, k))]

    for p in range(n):
        inverse = 1.0 / block[(p, p)]
        scaled = {q: at(block, q, p) * inverse for q in range(n) if q != p}
        new = {}
        for q in range(n):
            for k in range(q, n):
                if q == p and k == p:
                    new[(q, k)] = -inverse
                elif q == p:
                    new[(q, k)] = scaled[k]
                elif k == p:
                    new[(q, k)] = scaled[q]
                else:
                    new[(q, k)] = block[(q, k)] - scaled[q] * at(block, p, k)
        block = new
    return block


def tree_sum(terms):
    while len(terms) > 1:
        terms = [terms[i] + terms[i + 1] for i in range(0, len(terms), 2)]
    return terms[0]


def panel_rows(x):
    w, n = x.shape
    b = PIVOTS
    lane = lax.broadcasted_iota(jnp.int32, (b, n), 1)
    sub = lax.broadcasted_iota(jnp.int32, (b, n), 0)
    for p in range(0, w, b):
        inside = (lane >= p) & (lane < p + b)
        columns = [jnp.broadcast_to(x[:, p + k : p + k + 1], (w, n)) for k in range(b)]
        block = {
            (q, k): jnp.broadcast_to(columns[k][p + q : p + q + 1, :], (b, n))
            for q in range(b)
            for k in range(q, b)
        }
        minus_inverse = swept(block, b)
        top = jnp.where(inside, jnp.where(lane == sub + p, -1.0, 0.0), x[p : p + b, :])
        rows = [jnp.broadcast_to(top[k : k + 1, :], (b, n)) for k in range(b)]
        minus_new = [
            tree_sum([minus_inverse[(min(q, k), max(q, k))] * rows[k] for k in range(b)])
            for q in range(b)
        ]
        tiles = []
        for t in range(0, w, b):
            if t == p:
                tile = -minus_new[0]
                for q in range(1, b):
                    tile = jnp.where(sub == q, -minus_new[q], tile)
            else:
                tile = jnp.where(inside, 0.0, x[t : t + b, :]) + tree_sum(
                    [columns[k][t : t + b, :] * minus_new[k] for k in range(b)]
                )
            tiles.append(tile)
        x = jnp.concatenate(tiles, axis=0)
    return x


def half_swept(x):
    n = x.shape[0]
    new = panel_rows(x[0:PANEL, :])
    lane = lax.broadcasted_iota(jnp.int32, (n - PANEL, n), 1)
    rest = jnp.where(lane < PANEL, 0.0, x[PANEL:, :]) - dot(x[PANEL:, 0:PANEL], new)
    return pltpu.roll(jnp.concatenate([rest, new], axis=0), n - PANEL, 1)


def minus_inverse_of(x):
    return lax.fori_loop(0, x.shape[0] // PANEL, lambda _, held: half_swept(held), x)


def sweep_block(x_ref, new_ref, k):
    at = slice(k * B, (k + 1) * B)
    finish_block(x_ref, new_ref, k, minus_inverse_of(x_ref[at, at]))


def finish_block(x_ref, new_ref, k, minus):
    at = slice(k * B, (k + 1) * B)
    row = halves(x_ref[at, :])
    new_ref[...] = -dot3(minus, row)
    new_ref[:, at] = minus
    new = new_ref[...]
    right = halves(new)
    for i in range(NB):
        if i != k:
            rows = slice(i * B, (i + 1) * B)
            x_ref[rows, at] = jnp.zeros((B, B), jnp.float32)
            x_ref[rows, :] = x_ref[rows, :] - dot3(tuple(h[:, rows] for h in row), right, 0)
    x_ref[at, :] = new


def fill_symmetric(x_ref, row, blocks):
    diagonal = lax.broadcasted_iota(jnp.int32, (B, B), 0) == lax.broadcasted_iota(
        jnp.int32, (B, B), 1
    )
    eye = jnp.where(diagonal, 1.0, 0.0)
    for (i, j), at in TRI.items():
        if i not in row:
            continue
        value = blocks(at)
        ri, rj = slice(i * B, (i + 1) * B), slice(j * B, (j + 1) * B)
        if i == j:
            x_ref[ri, ri] = value + eye
        else:
            x_ref[ri, rj] = value
            x_ref[rj, ri] = value.T


def kernel(no, ny, nz, *refs):
    basis_ref, fields_ref, positions_ref, nugget_ref, mean_ref, root_ref = refs[:6]
    solved, padded = refs[6:8]
    local, first_in, held, second_in, full = (refs[8 + 5 * i : 13 + 5 * i] for i in range(5))
    knot, new_rows, weights, correction, outer_in, half_p, packed_p, root = refs[33:41]
    s1, r1, s2, r2, gs2, gr2, gs1, gr1, so, ro, psz, prz, psy, pry, psc, prc = refs[41:]
    o = lax.axis_index("outer")
    y = lax.axis_index("inner_0")
    z = lax.axis_index("inner_1")
    me = y * nz + z
    inner = ny * nz

    def y_peer(k):
        return {"inner_0": lax.rem(y + k, ny)}

    def z_peer(k):
        return {"inner_1": lax.rem(z + k, nz)}

    def o_peer(k):
        return {"outer": lax.rem(o + k, no)}

    def axes(part):
        in_y, in_z = (ny, y, y_peer), (nz, z, z_peer)
        return (in_z, in_y) if part in Z_FIRST else (in_y, in_z)

    peers = (
        [y_peer(k) for k in range(1, ny)]
        + [z_peer(k) for k in range(1, nz)]
        + [o_peer(k) for k in range(1, no)]
    )
    barrier = pltpu.get_barrier_semaphore()
    for peer in peers:
        pl.semaphore_signal(barrier, inc=1, device_id=peer, device_id_type=pl.DeviceIdType.MESH)

    sent = []

    def send(src, dst, send_sem, recv_sem, peer):
        copy = pltpu.make_async_remote_copy(
            src_ref=src,
            dst_ref=dst,
            send_sem=send_sem,
            recv_sem=recv_sem,
            device_id=peer,
            device_id_type=pl.DeviceIdType.MESH,
        )
        copy.start()
        sent.append(copy)
        return copy

    def span(index, rows):
        return pl.ds(pl.multiple_of(index * rows, 8), rows)

    def own(part):
        (n1, i1, _), (n2, i2, _) = axes(part)
        return span(i1 * n2 + i2, PART_ROWS[part] // inner)

    def summed(landing, mine):
        total = mine
        for k in range(landing.shape[0]):
            total = total + landing[k]
        return total

    def arrived(copies):
        for copy in copies:
            copy.wait_recv()

    pending = {}

    def sum_first(part):
        n, index, peer = axes(part)[0]
        rows = PART_ROWS[part] // n
        pending[part] = [
            send(
                local[part].at[span(lax.rem(index + k, n), rows)],
                first_in[part].at[k - 1],
                s1.at[part, k - 1],
                r1.at[part, k - 1],
                peer(k),
            )
            for k in range(1, n)
        ]

    def sum_second(part):
        n1, index1, _ = axes(part)[0]
        n, index, peer = axes(part)[1]
        arrived(pending[part])
        held[part][...] = summed(
            first_in[part], local[part][span(index1, PART_ROWS[part] // n1), :]
        )
        rows = PART_ROWS[part] // inner
        pending[part] = [
            send(
                held[part].at[span(lax.rem(index + k, n), rows)],
                second_in[part].at[k - 1],
                s2.at[part, k - 1],
                r2.at[part, k - 1],
                peer(k),
            )
            for k in range(1, n)
        ]

    def whole_sum(part):
        _, index, _ = axes(part)[1]
        arrived(pending[part])
        return summed(second_in[part], held[part][span(index, PART_ROWS[part] // inner), :])

    def gather_second(part):
        full[part][own(part), :] = whole_sum(part)
        n, _, peer = axes(part)[1]
        block = full[part].at[own(part)]
        pending[part] = [
            send(block, block, gs2.at[part, k - 1], gr2.at[part, k - 1], peer(k))
            for k in range(1, n)
        ]

    def gather_first(part):
        arrived(pending[part])
        n, index, peer = axes(part)[0]
        block = full[part].at[span(index, PART_ROWS[part] // n)]
        pending[part] = [
            send(block, block, gs1.at[part, k - 1], gr1.at[part, k - 1], peer(k))
            for k in range(1, n)
        ]

    def gathered(part):
        arrived(pending[part])

    def basis_block(i):
        return basis_ref[:, i * B : (i + 1) * B]

    def cross(ref_early, ref_late, k, j):
        block = k * NB + j
        late = block - NB * NB // 2
        ref, at = (ref_late, late) if late >= 0 else (ref_early, block)
        return ref.at[at * B : (at + 1) * B]

    def rhs(ref_early, k):
        at = NB * NB // 2 + k
        return ref_early.at[at * B : (at + 1) * B]

    position = jnp.broadcast_to(positions_ref[...].astype(jnp.float32), (B, B))
    diagonal = lax.broadcasted_iota(jnp.int32, (B, B), 0) == lax.broadcasted_iota(
        jnp.int32, (B, B), 1
    )
    covariance = jnp.exp(-jnp.abs(position - position.T) / RANGE) + jnp.where(
        diagonal, jnp.broadcast_to(nugget_ref[...], (B, B)), 0.0
    )
    minus = minus_inverse_of(covariance)
    solved[:, 0:M] = -dot3(minus, basis_ref[:, 0:M])
    row = dot3(basis_block(0), solved[:, 0:M], 0)
    for j in range(NB):
        local[TOP][j * B : (j + 1) * B, :] = row[:, j * B : (j + 1) * B]
    pl.semaphore_wait(barrier, len(peers))
    sum_first(TOP)
    for i in range(1, NB):
        row = dot3(basis_block(i), solved[:, i * B : M], 0)
        for j in range(i, NB):
            at = (TRI[(i, j)] - NB) * B
            local[REST][at : at + B, :] = row[:, (j - i) * B : (j - i + 1) * B]
    sum_first(REST)
    solved[:, M:] = -dot3(minus, basis_ref[:, M:])
    padded[...] = jnp.zeros_like(padded)
    padded[:, 0:F] = fields_ref[...]
    left_fields = -dot3(minus, padded[...])
    right_fields = pltpu.roll(left_fields, F, 1)

    def cross_rows(k):
        row = dot3(basis_block(k), solved[:, M:], 0)
        for j in range(NB):
            cross(local[EARLY], local[LATE], k, j)[...] = row[:, j * B : (j + 1) * B]

    for k in range(NB // 2):
        cross_rows(k)
    for i in range(NB):
        rhs(local[EARLY], i)[...] = dot3(basis_block(i), left_fields, 0) + dot3(
            basis_block(NB + i), right_fields, 0
        )
    sum_second(TOP)
    sum_first(EARLY)
    for k in range(NB // 2, NB):
        cross_rows(k)
    gather_second(TOP)
    sum_second(REST)
    gather_first(TOP)
    for i in range(NB):
        row = dot3(basis_block(NB + i), solved[:, M + i * B :], 0)
        for j in range(i, NB):
            at = TRI[(i, j)] * B
            local[ROOT][at : at + B, :] = row[:, (j - i) * B : (j - i + 1) * B]
    gather_second(REST)
    sum_first(LATE)
    gathered(TOP)

    fill_symmetric(knot, (0,), lambda at: full[TOP][at * B : (at + 1) * B, :])
    minus = half_swept(knot[0:B, 0:B])
    gather_first(REST)
    sum_second(EARLY)
    sum_first(ROOT)
    minus = half_swept(minus)
    gathered(REST)
    fill_symmetric(
        knot, (1, 2, 3), lambda at: full[REST][(at - NB) * B : (at - NB + 1) * B, :]
    )
    finish_block(knot, new_rows, 0, minus)
    minus = half_swept(knot[B : 2 * B, B : 2 * B])
    sum_second(LATE)
    gather_second(EARLY)
    minus = half_swept(minus)
    finish_block(knot, new_rows, 1, minus)
    gather_second(LATE)
    gather_first(EARLY)
    minus = half_swept(knot[2 * B : 3 * B, 2 * B : 3 * B])
    gather_first(LATE)
    sum_second(ROOT)
    minus = half_swept(minus)
    finish_block(knot, new_rows, 2, minus)
    minus = half_swept(knot[3 * B :, 3 * B :])
    minus = half_swept(minus)
    finish_block(knot, new_rows, 3, minus)
    gathered(EARLY)
    gathered(LATE)

    def cross_at(k, j):
        return cross(full[EARLY], full[LATE], k, j)[...]

    def rhs_at(k):
        return rhs(full[EARLY], k)[...]

    right = halves(
        jnp.concatenate(
            [
                jnp.concatenate([cross_at(k, j) for j in range(NB)] + [rhs_at(k)], axis=1)
                for k in range(NB)
            ],
            axis=0,
        )
    )
    weights[...] = -dot3(knot[...], right)
    solved_cross = halves(weights[...])
    reduced = []
    for i in range(NB):
        total = dot3(
            tuple(h[:, i * B : (i + 1) * B] for h in right),
            tuple(h[:, i * B :] for h in solved_cross),
            0,
        )
        for j in range(i, NB):
            at = TRI[(i, j)] * B
            correction[at : at + B, :] = total[:, (j - i) * B : (j - i + 1) * B]
        reduced.append(pltpu.roll(rhs_at(i), F, 1) - total[:, (NB - i) * B :])
    lane = lax.broadcasted_iota(jnp.int32, (B, B), 1)
    for i in range(NB // 2):
        at = TRI_ROWS + i * B
        correction[at : at + B, :] = jnp.where(
            lane < F, reduced[i], pltpu.roll(reduced[i + NB // 2], F, 1)
        )
    a_share, r_share = TRI_ROWS // inner, RED_ROWS // inner
    share = a_share + r_share
    outer_in[o, 0:a_share, :] = whole_sum(ROOT) - correction[span(me, a_share), :]
    outer_in[o, a_share:share, :] = correction[
        pl.ds(pl.multiple_of(TRI_ROWS + me * r_share, 8), r_share), :
    ]
    arrived(
        [
            send(outer_in.at[o], outer_in.at[o], so.at[k - 1], ro.at[k - 1], o_peer(k))
            for k in range(1, no)
        ]
    )

    core = lax.rem(o, 2)
    sibling = {"outer": o + 1 - 2 * core}
    h = share // 2
    mine = pl.ds(pl.multiple_of(core * h, 8), h)
    total = outer_in[0, mine, :]
    for k in range(1, no):
        total = total + outer_in[k, mine, :]
    half_p[core, span(me, h), :] = total
    block = half_p.at[core, span(me, h)]
    arrived(
        [
            send(block, block, psz.at[k - 1], prz.at[k - 1], z_peer(k))
            for k in range(1, nz)
        ]
    )
    block = half_p.at[core, span(y, h * nz)]
    over_y = [
        send(block, block, psy.at[k - 1], pry.at[k - 1], y_peer(k)) for k in range(1, ny)
    ]
    swaps = [send(block, block, psc.at[0], prc.at[0], sibling)]
    for k in range(1, ny):
        over_y[k - 1].wait_recv()
        block = half_p.at[core, span(lax.rem(y + ny - k, ny), h * nz)]
        swaps.append(send(block, block, psc.at[k], prc.at[k], sibling))
    arrived(swaps)
    for d in range(inner):
        for c in range(2):
            lo, hi = c * h, min((c + 1) * h, a_share)
            packed_p[d * a_share + lo : d * a_share + hi, :] = half_p[
                c, d * h : d * h + hi - lo, :
            ]
        at = TRI_ROWS + d * r_share
        packed_p[at : at + r_share, :] = half_p[1, (d + 1) * h - r_share : (d + 1) * h, :]

    fill_symmetric(root, range(NB), lambda at: packed_p[at * B : (at + 1) * B, :])
    for k in range(NB):
        sweep_block(root, new_rows, k)
    half = packed_p[TRI_ROWS:, :]
    root_coef = -dot3(root[...], jnp.concatenate([half, pltpu.roll(half, F, 1)], axis=0))
    root_ref[...] = root_coef[:, 0:F]
    region_coef = weights[:, M:] - dot3(weights[:, 0:M], root_coef)
    mean = dot3(basis_ref[:, 0:M], region_coef) + dot3(basis_ref[:, M:], root_coef)
    mean_ref[...] = mean[:, 0:F]
    for copy in sent:
        copy.wait_send()


def shards(basis, fields, positions, nugget):
    no, ny, nz = (lax.axis_size(axis) for axis in OUTER_INNER)
    inner = ny * nz
    f32 = jnp.float32

    def landing(parts, rows):
        return pltpu.VMEM((parts, rows, B), f32)

    def flat(rows):
        return pltpu.VMEM((rows, B), f32)

    share = (TRI_ROWS + RED_ROWS) // inner
    dma = pltpu.SemaphoreType.DMA
    parts = list(PART_ROWS.items())
    first = [nz if part in Z_FIRST else ny for part, _ in parts]
    widest = max(ny, nz) - 1
    scratch = (
        [pltpu.VMEM((B, K), f32), flat(B)]
        + [flat(rows) for _, rows in parts]
        + [landing(n - 1, rows // n) for n, (_, rows) in zip(first, parts)]
        + [flat(rows // n) for n, (_, rows) in zip(first, parts)]
        + [landing(inner // n - 1, rows // inner) for n, (_, rows) in zip(first, parts)]
        + [flat(rows if part != ROOT else B) for part, rows in parts]
        + [pltpu.VMEM((M, M), f32), pltpu.VMEM((B, M), f32), pltpu.VMEM((M, M + B), f32)]
        + [flat(TRI_ROWS + RED_ROWS), landing(no, share), landing(2, share // 2 * inner)]
        + [flat(TRI_ROWS + RED_ROWS), pltpu.VMEM((R, R), f32)]
        + [dma((len(parts), widest))] * 8
        + [dma((no - 1,))] * 2
        + [dma((nz - 1,))] * 2
        + [dma((ny - 1,))] * 2
        + [dma((ny,))] * 2
    )
    return pl.pallas_call(
        functools.partial(kernel, no, ny, nz),
        out_shape=(
            jax.ShapeDtypeStruct((B, F), f32),
            jax.ShapeDtypeStruct((R, F), f32),
        ),
        in_specs=[pl.BlockSpec(memory_space=pltpu.VMEM)] * 4,
        out_specs=(pl.BlockSpec(memory_space=pltpu.VMEM),) * 2,
        scratch_shapes=scratch,
        compiler_params=pltpu.CompilerParams(
            collective_id=0, has_side_effects=True, vmem_limit_bytes=48 * 1024 * 1024
        ),
    )(basis, fields, positions.reshape(1, B), nugget.reshape(1, B))


def solution(mesh):
    split = Mesh(mesh.devices.reshape(mesh.shape["outer"], 4, 8), ("outer", "inner_0", "inner_1"))
    in_specs = (P(OUTER_INNER, None), P(OUTER_INNER, None), P(OUTER_INNER), P(OUTER_INNER))
    out_specs = (P(OUTER_INNER, None), P())
    return jax.shard_map(
        shards, mesh=split, in_specs=in_specs, out_specs=out_specs, check_vma=False
    )
```

```python
import functools

import jax
import jax.numpy as jnp
from jax import lax
from jax.experimental import pallas as pl
from jax.experimental.pallas import tpu as pltpu
from jax.sharding import Mesh
from jax.sharding import PartitionSpec as P

M = 512
R = 512
K = 1024
F = 64
RANGE = 8
B = 128
PIVOTS = 8
PANEL = 64
NB = M // B
OUTER_INNER = ("outer", "inner_0", "inner_1")
PAIRS = [(i, j) for i in range(NB) for j in range(i, NB)]
TRI = {pair: at for at, pair in enumerate(PAIRS)}
TRI_ROWS = len(PAIRS) * B
RED_ROWS = R // 2
TOP, REST, EARLY, LATE, ROOT = range(5)
PART_ROWS = {
    TOP: NB * B,
    REST: TRI_ROWS - NB * B,
    EARLY: (NB * NB // 2 + NB) * B,
    LATE: NB * NB // 2 * B,
    ROOT: TRI_ROWS,
}
Z_FIRST = (LATE,)


def dot(left, right, left_dim=1):
    return lax.dot_general(
        left,
        right,
        (((left_dim,), (0,)), ((), ())),
        precision=lax.Precision.HIGHEST,
        preferred_element_type=jnp.float32,
    )


def halves(x):
    high = x.astype(jnp.bfloat16)
    return high, (x - high.astype(jnp.float32)).astype(jnp.bfloat16)


def dot3(left, right, left_dim=1):
    left = left if isinstance(left, tuple) else halves(left)
    right = right if isinstance(right, tuple) else halves(right)

    def one(a, b):
        return lax.dot_general(
            a, b, (((left_dim,), (0,)), ((), ())), preferred_element_type=jnp.float32
        )

    return one(left[0], right[0]) + (one(left[0], right[1]) + one(left[1], right[0]))


def swept(block, n):
    def at(values, q, k):
        return values[(min(q, k), max(q, k))]

    for p in range(n):
        inverse = 1.0 / block[(p, p)]
        scaled = {q: at(block, q, p) * inverse for q in range(n) if q != p}
        new = {}
        for q in range(n):
            for k in range(q, n):
                if q == p and k == p:
                    new[(q, k)] = -inverse
                elif q == p:
                    new[(q, k)] = scaled[k]
                elif k == p:
                    new[(q, k)] = scaled[q]
                else:
                    new[(q, k)] = block[(q, k)] - scaled[q] * at(block, p, k)
        block = new
    return block


def tree_sum(terms):
    while len(terms) > 1:
        terms = [terms[i] + terms[i + 1] for i in range(0, len(terms), 2)]
    return terms[0]


def panel_rows(x):
    w, n = x.shape
    b = PIVOTS
    lane = lax.broadcasted_iota(jnp.int32, (b, n), 1)
    sub = lax.broadcasted_iota(jnp.int32, (b, n), 0)
    for p in range(0, w, b):
        inside = (lane >= p) & (lane < p + b)
        columns = [jnp.broadcast_to(x[:, p + k : p + k + 1], (w, n)) for k in range(b)]
        block = {
            (q, k): jnp.broadcast_to(columns[k][p + q : p + q + 1, :], (b, n))
            for q in range(b)
            for k in range(q, b)
        }
        minus_inverse = swept(block, b)
        top = jnp.where(inside, jnp.where(lane == sub + p, -1.0, 0.0), x[p : p + b, :])
        rows = [jnp.broadcast_to(top[k : k + 1, :], (b, n)) for k in range(b)]
        minus_new = [
            tree_sum([minus_inverse[(min(q, k), max(q, k))] * rows[k] for k in range(b)])
            for q in range(b)
        ]
        tiles = []
        for t in range(0, w, b):
            if t == p:
                tile = -minus_new[0]
                for q in range(1, b):
                    tile = jnp.where(sub == q, -minus_new[q], tile)
            else:
                tile = jnp.where(inside, 0.0, x[t : t + b, :]) + tree_sum(
                    [columns[k][t : t + b, :] * minus_new[k] for k in range(b)]
                )
            tiles.append(tile)
        x = jnp.concatenate(tiles, axis=0)
    return x


def half_swept(x):
    n = x.shape[0]
    new = panel_rows(x[0:PANEL, :])
    lane = lax.broadcasted_iota(jnp.int32, (n - PANEL, n), 1)
    rest = jnp.where(lane < PANEL, 0.0, x[PANEL:, :]) - dot(x[PANEL:, 0:PANEL], new)
    return pltpu.roll(jnp.concatenate([rest, new], axis=0), n - PANEL, 1)


def minus_inverse_of(x):
    return lax.fori_loop(0, x.shape[0] // PANEL, lambda _, held: half_swept(held), x)


def sweep_block(x_ref, new_ref, k):
    at = slice(k * B, (k + 1) * B)
    finish_block(x_ref, new_ref, k, minus_inverse_of(x_ref[at, at]))


def finish_block(x_ref, new_ref, k, minus):
    at = slice(k * B, (k + 1) * B)
    row = halves(x_ref[at, :])
    new_ref[...] = -dot3(minus, row)
    new_ref[:, at] = minus
    new = new_ref[...]
    right = halves(new)
    for i in range(NB):
        if i != k:
            rows = slice(i * B, (i + 1) * B)
            x_ref[rows, at] = jnp.zeros((B, B), jnp.float32)
            x_ref[rows, :] = x_ref[rows, :] - dot3(tuple(h[:, rows] for h in row), right, 0)
    x_ref[at, :] = new


def fill_symmetric(x_ref, row, blocks):
    diagonal = lax.broadcasted_iota(jnp.int32, (B, B), 0) == lax.broadcasted_iota(
        jnp.int32, (B, B), 1
    )
    eye = jnp.where(diagonal, 1.0, 0.0)
    for (i, j), at in TRI.items():
        if i not in row:
            continue
        value = blocks(at)
        ri, rj = slice(i * B, (i + 1) * B), slice(j * B, (j + 1) * B)
        if i == j:
            x_ref[ri, ri] = value + eye
        else:
            x_ref[ri, rj] = value
            x_ref[rj, ri] = value.T


def kernel(no, ny, nz, *refs):
    basis_far, fields_far, positions_ref, nugget_ref, mean_ref, root_ref = refs[:6]
    solved, padded = refs[6:8]
    local, first_in, held, second_in, full = (refs[8 + 5 * i : 13 + 5 * i] for i in range(5))
    knot, new_rows, weights, correction, outer_in, half_p, packed_p, root = refs[33:41]
    s1, r1, s2, r2, gs2, gr2, gs1, gr1, so, ro, psz, prz, psy, pry, psc, prc = refs[41:57]
    basis_ref, fields_ref, loaded = refs[57:]
    loads = [
        pltpu.make_async_copy(basis_far, basis_ref, loaded.at[0]),
        pltpu.make_async_copy(fields_far, fields_ref, loaded.at[1]),
    ]
    for load in loads:
        load.start()
    o = lax.axis_index("outer")
    y = lax.axis_index("inner_0")
    z = lax.axis_index("inner_1")
    me = y * nz + z
    inner = ny * nz

    def y_peer(k):
        return {"inner_0": lax.rem(y + k, ny)}

    def z_peer(k):
        return {"inner_1": lax.rem(z + k, nz)}

    def o_peer(k):
        return {"outer": lax.rem(o + k, no)}

    def axes(part):
        in_y, in_z = (ny, y, y_peer), (nz, z, z_peer)
        return (in_z, in_y) if part in Z_FIRST else (in_y, in_z)

    peers = (
        [y_peer(k) for k in range(1, ny)]
        + [z_peer(k) for k in range(1, nz)]
        + [o_peer(k) for k in range(1, no)]
    )
    barrier = pltpu.get_barrier_semaphore()
    for peer in peers:
        pl.semaphore_signal(barrier, inc=1, device_id=peer, device_id_type=pl.DeviceIdType.MESH)

    sent = []

    def send(src, dst, send_sem, recv_sem, peer):
        copy = pltpu.make_async_remote_copy(
            src_ref=src,
            dst_ref=dst,
            send_sem=send_sem,
            recv_sem=recv_sem,
            device_id=peer,
            device_id_type=pl.DeviceIdType.MESH,
        )
        copy.start()
        sent.append(copy)
        return copy

    def span(index, rows):
        return pl.ds(pl.multiple_of(index * rows, 8), rows)

    def own(part):
        (n1, i1, _), (n2, i2, _) = axes(part)
        return span(i1 * n2 + i2, PART_ROWS[part] // inner)

    def summed(landing, mine):
        total = mine
        for k in range(landing.shape[0]):
            total = total + landing[k]
        return total

    def arrived(copies):
        for copy in copies:
            copy.wait_recv()

    pending = {}

    def sum_first(part):
        n, index, peer = axes(part)[0]
        rows = PART_ROWS[part] // n
        pending[part] = [
            send(
                local[part].at[span(lax.rem(index + k, n), rows)],
                first_in[part].at[k - 1],
                s1.at[part, k - 1],
                r1.at[part, k - 1],
                peer(k),
            )
            for k in range(1, n)
        ]

    def sum_second(part):
        n1, index1, _ = axes(part)[0]
        n, index, peer = axes(part)[1]
        arrived(pending[part])
        held[part][...] = summed(
            first_in[part], local[part][span(index1, PART_ROWS[part] // n1), :]
        )
        rows = PART_ROWS[part] // inner
        pending[part] = [
            send(
                held[part].at[span(lax.rem(index + k, n), rows)],
                second_in[part].at[k - 1],
                s2.at[part, k - 1],
                r2.at[part, k - 1],
                peer(k),
            )
            for k in range(1, n)
        ]

    def whole_sum(part):
        _, index, _ = axes(part)[1]
        arrived(pending[part])
        return summed(second_in[part], held[part][span(index, PART_ROWS[part] // inner), :])

    def gather_second(part):
        full[part][own(part), :] = whole_sum(part)
        n, _, peer = axes(part)[1]
        block = full[part].at[own(part)]
        pending[part] = [
            send(block, block, gs2.at[part, k - 1], gr2.at[part, k - 1], peer(k))
            for k in range(1, n)
        ]

    def gather_first(part):
        arrived(pending[part])
        n, index, peer = axes(part)[0]
        block = full[part].at[span(index, PART_ROWS[part] // n)]
        pending[part] = [
            send(block, block, gs1.at[part, k - 1], gr1.at[part, k - 1], peer(k))
            for k in range(1, n)
        ]

    def gathered(part):
        arrived(pending[part])

    def basis_block(i):
        return basis_ref[:, i * B : (i + 1) * B]

    def cross(ref_early, ref_late, k, j):
        block = k * NB + j
        late = block - NB * NB // 2
        ref, at = (ref_late, late) if late >= 0 else (ref_early, block)
        return ref.at[at * B : (at + 1) * B]

    def rhs(ref_early, k):
        at = NB * NB // 2 + k
        return ref_early.at[at * B : (at + 1) * B]

    position = jnp.broadcast_to(positions_ref[...].astype(jnp.float32), (B, B))
    diagonal = lax.broadcasted_iota(jnp.int32, (B, B), 0) == lax.broadcasted_iota(
        jnp.int32, (B, B), 1
    )
    covariance = jnp.exp(-jnp.abs(position - position.T) / RANGE) + jnp.where(
        diagonal, jnp.broadcast_to(nugget_ref[...], (B, B)), 0.0
    )
    minus = minus_inverse_of(covariance)
    for load in loads:
        load.wait()
    solved[:, 0:M] = -dot3(minus, basis_ref[:, 0:M])
    row = dot3(basis_block(0), solved[:, 0:M], 0)
    for j in range(NB):
        local[TOP][j * B : (j + 1) * B, :] = row[:, j * B : (j + 1) * B]
    pl.semaphore_wait(barrier, len(peers))
    sum_first(TOP)
    for i in range(1, NB):
        row = dot3(basis_block(i), solved[:, i * B : M], 0)
        for j in range(i, NB):
            at = (TRI[(i, j)] - NB) * B
            local[REST][at : at + B, :] = row[:, (j - i) * B : (j - i + 1) * B]
    sum_first(REST)
    solved[:, M:] = -dot3(minus, basis_ref[:, M:])
    padded[...] = jnp.zeros_like(padded)
    padded[0:F, :] = fields_ref[...]
    left_fields = -dot3(minus, padded[...].T)
    right_fields = pltpu.roll(left_fields, F, 1)

    def cross_rows(k):
        row = dot3(basis_block(k), solved[:, M:], 0)
        for j in range(NB):
            cross(local[EARLY], local[LATE], k, j)[...] = row[:, j * B : (j + 1) * B]

    for k in range(NB // 2):
        cross_rows(k)
    for i in range(NB):
        rhs(local[EARLY], i)[...] = dot3(basis_block(i), left_fields, 0) + dot3(
            basis_block(NB + i), right_fields, 0
        )
    sum_second(TOP)
    sum_first(EARLY)
    for k in range(NB // 2, NB):
        cross_rows(k)
    gather_second(TOP)
    sum_second(REST)
    gather_first(TOP)
    for i in range(NB):
        row = dot3(basis_block(NB + i), solved[:, M + i * B :], 0)
        for j in range(i, NB):
            at = TRI[(i, j)] * B
            local[ROOT][at : at + B, :] = row[:, (j - i) * B : (j - i + 1) * B]
    gather_second(REST)
    sum_first(LATE)
    gathered(TOP)

    fill_symmetric(knot, (0,), lambda at: full[TOP][at * B : (at + 1) * B, :])
    minus = half_swept(knot[0:B, 0:B])
    gather_first(REST)
    sum_second(EARLY)
    sum_first(ROOT)
    minus = half_swept(minus)
    gathered(REST)
    fill_symmetric(
        knot, (1, 2, 3), lambda at: full[REST][(at - NB) * B : (at - NB + 1) * B, :]
    )
    finish_block(knot, new_rows, 0, minus)
    sum_second(LATE)
    gather_second(EARLY)
    minus = half_swept(knot[B : 2 * B, B : 2 * B])
    gather_second(LATE)
    gather_first(EARLY)
    minus = half_swept(minus)
    finish_block(knot, new_rows, 1, minus)
    gather_first(LATE)
    sum_second(ROOT)
    for k in range(2, NB):
        sweep_block(knot, new_rows, k)
    def cross_at(k, j):
        return cross(full[EARLY], full[LATE], k, j)[...]

    def rhs_at(k):
        return rhs(full[EARLY], k)[...]

    def rows_of(ks):
        return halves(
            jnp.concatenate(
                [
                    jnp.concatenate([cross_at(k, j) for j in range(NB)] + [rhs_at(k)], axis=1)
                    for k in ks
                ],
                axis=0,
            )
        )

    gathered(EARLY)
    upper = rows_of(range(NB // 2))
    weights[...] = -dot3(knot[:, 0 : M // 2], upper)
    gathered(LATE)
    lower = rows_of(range(NB // 2, NB))
    weights[...] = weights[...] - dot3(knot[:, M // 2 :], lower)
    right = tuple(jnp.concatenate(pair, axis=0) for pair in zip(upper, lower))
    solved_cross = halves(weights[...])
    reduced = []
    for i in range(NB):
        total = dot3(
            tuple(h[:, i * B : (i + 1) * B] for h in right),
            tuple(h[:, i * B :] for h in solved_cross),
            0,
        )
        for j in range(i, NB):
            at = TRI[(i, j)] * B
            correction[at : at + B, :] = total[:, (j - i) * B : (j - i + 1) * B]
        reduced.append(pltpu.roll(rhs_at(i), F, 1) - total[:, (NB - i) * B :])
    lane = lax.broadcasted_iota(jnp.int32, (B, B), 1)
    for i in range(NB // 2):
        at = TRI_ROWS + i * B
        correction[at : at + B, :] = jnp.where(
            lane < F, reduced[i], pltpu.roll(reduced[i + NB // 2], F, 1)
        )
    a_share, r_share = TRI_ROWS // inner, RED_ROWS // inner
    share = a_share + r_share
    outer_in[o, 0:a_share, :] = whole_sum(ROOT) - correction[span(me, a_share), :]
    outer_in[o, a_share:share, :] = correction[
        pl.ds(pl.multiple_of(TRI_ROWS + me * r_share, 8), r_share), :
    ]
    arrived(
        [
            send(outer_in.at[o], outer_in.at[o], so.at[k - 1], ro.at[k - 1], o_peer(k))
            for k in range(1, no)
        ]
    )

    core = lax.rem(o, 2)
    sibling = {"outer": o + 1 - 2 * core}
    h = share // 2
    mine = pl.ds(pl.multiple_of(core * h, 8), h)
    total = outer_in[0, mine, :]
    for k in range(1, no):
        total = total + outer_in[k, mine, :]
    half_p[core, span(me, h), :] = total
    block = half_p.at[core, span(me, h)]
    arrived(
        [
            send(block, block, psz.at[k - 1], prz.at[k - 1], z_peer(k))
            for k in range(1, nz)
        ]
    )
    block = half_p.at[core, span(y, h * nz)]
    over_y = [
        send(block, block, psy.at[k - 1], pry.at[k - 1], y_peer(k)) for k in range(1, ny)
    ]
    swaps = [send(block, block, psc.at[0], prc.at[0], sibling)]
    for k in range(1, ny):
        over_y[k - 1].wait_recv()
        block = half_p.at[core, span(lax.rem(y + ny - k, ny), h * nz)]
        swaps.append(send(block, block, psc.at[k], prc.at[k], sibling))
    arrived(swaps)
    for d in range(inner):
        for c in range(2):
            lo, hi = c * h, min((c + 1) * h, a_share)
            packed_p[d * a_share + lo : d * a_share + hi, :] = half_p[
                c, d * h : d * h + hi - lo, :
            ]
        at = TRI_ROWS + d * r_share
        packed_p[at : at + r_share, :] = half_p[1, (d + 1) * h - r_share : (d + 1) * h, :]

    fill_symmetric(root, range(NB), lambda at: packed_p[at * B : (at + 1) * B, :])
    for k in range(NB):
        sweep_block(root, new_rows, k)
    half = packed_p[TRI_ROWS:, :]
    root_coef = -dot3(root[...], jnp.concatenate([half, pltpu.roll(half, F, 1)], axis=0))
    for i in range(NB):
        root_ref[:, i * B : (i + 1) * B] = root_coef[i * B : (i + 1) * B, :].T[0:F, :]
    region_coef = weights[:, M:] - dot3(weights[:, 0:M], root_coef)
    mean = dot3(basis_ref[:, 0:M], region_coef) + dot3(basis_ref[:, M:], root_coef)
    mean_ref[...] = mean.T[0:F, :]
    for copy in sent:
        copy.wait_send()


def shards(basis, fields, positions, nugget):
    no, ny, nz = (lax.axis_size(axis) for axis in OUTER_INNER)
    inner = ny * nz
    f32 = jnp.float32

    def landing(parts, rows):
        return pltpu.VMEM((parts, rows, B), f32)

    def flat(rows):
        return pltpu.VMEM((rows, B), f32)

    share = (TRI_ROWS + RED_ROWS) // inner
    dma = pltpu.SemaphoreType.DMA
    parts = list(PART_ROWS.items())
    first = [nz if part in Z_FIRST else ny for part, _ in parts]
    widest = max(ny, nz) - 1
    scratch = (
        [pltpu.VMEM((B, K), f32), flat(B)]
        + [flat(rows) for _, rows in parts]
        + [landing(n - 1, rows // n) for n, (_, rows) in zip(first, parts)]
        + [flat(rows // n) for n, (_, rows) in zip(first, parts)]
        + [landing(inner // n - 1, rows // inner) for n, (_, rows) in zip(first, parts)]
        + [flat(rows if part != ROOT else B) for part, rows in parts]
        + [pltpu.VMEM((M, M), f32), pltpu.VMEM((B, M), f32), pltpu.VMEM((M, M + B), f32)]
        + [flat(TRI_ROWS + RED_ROWS), landing(no, share), landing(2, share // 2 * inner)]
        + [flat(TRI_ROWS + RED_ROWS), pltpu.VMEM((R, R), f32)]
        + [dma((len(parts), widest))] * 8
        + [dma((no - 1,))] * 2
        + [dma((nz - 1,))] * 2
        + [dma((ny - 1,))] * 2
        + [dma((ny,))] * 2
        + [pltpu.VMEM((B, K), f32), pltpu.VMEM((F, B), f32), dma((2,))]
    )
    mean, root_coef = pl.pallas_call(
        functools.partial(kernel, no, ny, nz),
        out_shape=(
            jax.ShapeDtypeStruct((F, B), f32),
            jax.ShapeDtypeStruct((F, R), f32),
        ),
        in_specs=[pl.BlockSpec(memory_space=pltpu.HBM)] * 2
        + [pl.BlockSpec(memory_space=pltpu.VMEM)] * 2,
        out_specs=(pl.BlockSpec(memory_space=pltpu.VMEM),) * 2,
        scratch_shapes=scratch,
        compiler_params=pltpu.CompilerParams(
            collective_id=0, has_side_effects=True, vmem_limit_bytes=60 * 1024 * 1024
        ),
    )(basis, fields.T, positions.reshape(1, B), nugget.reshape(1, B))
    return mean.T, root_coef.T


def solution(mesh):
    split = Mesh(mesh.devices.reshape(mesh.shape["outer"], 4, 8), ("outer", "inner_0", "inner_1"))
    in_specs = (P(OUTER_INNER, None), P(OUTER_INNER, None), P(OUTER_INNER), P(OUTER_INNER))
    out_specs = (P(OUTER_INNER, None), P())
    return jax.shard_map(
        shards, mesh=split, in_specs=in_specs, out_specs=out_specs, check_vma=False
    )
```
